32 devices in a mesh: seq: 2 (over x), fsdp: 16 (over z, y, core).
Axes of the slice: x: 2, y: 2, z: 4, core: 2. Of those that a mesh axis runs over, the one named last changes fastest.
Arguments:
- tokens: bfloat16 [16, 256, 2048], P('fsdp', 'seq'), may hold values from -6 to 6
- norm_gain: bfloat16 [2048], P(('seq', 'fsdp')), may hold values from 0.5 to 1.5
- query_proj: bfloat16 [2048, 3072], P(('seq', 'fsdp')), may hold values from -0.125 to 0.125
- latent_proj: bfloat16 [2048, 576], P(('seq', 'fsdp')), may hold values from -0.125 to 0.125
- latent_gain: bfloat16 [512], P(('seq', 'fsdp')), may hold values from 0.5 to 1.5
- expand_proj: bfloat16 [512, 4096], P(('seq', 'fsdp')), may hold values from -0.25 to 0.25
- output_proj: bfloat16 [2048, 2048], P(('seq', 'fsdp')), may hold values from -0.5 to 0.5
- mixer_gain: bfloat16 [2048], P(('seq', 'fsdp')), may hold values from 0.5 to 1.5
- shared_gate: bfloat16 [2048, 2816], P(('seq', 'fsdp')), may hold values from -0.125 to 0.125
- shared_up: bfloat16 [2048, 2816], P(('seq', 'fsdp')), may hold values from -0.125 to 0.125
- shared_down: bfloat16 [2816, 2048], P(('seq', 'fsdp')), may hold values from -0.15625 to 0.15625
- expert_gate: bfloat16 [16, 2048, 1408], P('fsdp', None, 'seq'), may hold values from -0.125 to 0.125
- expert_up: bfloat16 [16, 2048, 1408], P('fsdp', None, 'seq'), may hold values from -0.125 to 0.125
- expert_down: bfloat16 [16, 1408, 2048], P('fsdp', 'seq'), may hold values from -0.4375 to 0.4375
- doc_starts: int32 [16, 256], P('fsdp'), may hold values from 0 to 1, as said below
- routes: int32 [16, 256, 6], P('fsdp', 'seq'), may hold values from 0 to 15, all different within a row; in each aligned block of 128 rows (0 to 127, 128 to 255, ..., all dimensions but the last counted through in order) at most 72 rows name the same one
- gate_levels: int32 [16, 256, 6], P('fsdp', 'seq'), may hold values from 1 to 8
- cotangent: bfloat16 [16, 256, 2048], P('fsdp', 'seq'), may hold values from -6 to 6
Outputs:
- layer_out: float32 [16, 256, 2048], P('fsdp', 'seq')
- input_grad: float32 [16, 256, 2048], P('fsdp', 'seq')
- norm_gain_grad: float32 [2048], P(('seq', 'fsdp'))
- query_proj_grad: float32 [2048, 3072], P(('seq', 'fsdp'))
- latent_proj_grad: float32 [2048, 576], P(('seq', 'fsdp'))
- latent_gain_grad: float32 [512], P(('seq', 'fsdp'))
- expand_proj_grad: float32 [512, 4096], P(('seq', 'fsdp'))
- output_proj_grad: float32 [2048, 2048], P(('seq', 'fsdp'))
- mixer_gain_grad: float32 [2048], P(('seq', 'fsdp'))
- shared_gate_grad: float32 [2048, 2816], P(('seq', 'fsdp'))
- shared_up_grad: float32 [2048, 2816], P(('seq', 'fsdp'))
- shared_down_grad: float32 [2816, 2048], P(('seq', 'fsdp'))
- expert_gate_grad: float32 [16, 2048, 1408], P('fsdp', None, 'seq')
- expert_up_grad: float32 [16, 2048, 1408], P('fsdp', None, 'seq')
- expert_down_grad: float32 [16, 1408, 2048], P('fsdp', 'seq')
The draws below stay inside these ranges and needn't reach their ends.
Inputs may be any that keep to these rules, and one draw needn't show every extreme that they name: `doc_starts`: every sequence starts a document at position 0 and has at most one more start, after position 160. `routes`: A token names 6 different experts; among the 128 rows of one device no expert is named more than 72 times, a bound that some block reaches.
All inputs are finite; a program needn't handle non-finite values.
Results may differ from the reference program's by a relative error of at most 0.018.
Values may be sent and summed in bfloat16 or wider, within the bound.
A program may use at most 384 MiB of HBM per device.

```python
import math
import jax
import jax.numpy as jnp
import numpy as np
from jax import lax

D = 2048
H = 16
DN = 128
DR = 64
DV = 128
KVL = 512
FF = 1408
SFF = 2816
TOPK = 6
TOK_DEV = 128
LEN = 256
NSEQ = 16
EXPERTS = 16
CAP = 72
N_SEQ = 2
N_FSDP = 16


def draw_doc_starts(key, part):
    key = jax.random.fold_in(key, 11)
    spot_key, flag_key = jax.random.split(key)
    earliest = LEN // 2 + LEN // 8 + 1
    spots = jax.random.randint(spot_key, (NSEQ,), earliest, LEN)
    flags = jax.random.randint(flag_key, (NSEQ,), 0, 2)
    positions = jnp.arange(LEN)[None, :]
    second = (positions == spots[:, None]) & (flags[:, None] == 1)
    markers = (positions == 0) | second
    return markers.astype(jnp.int32)


def set_ends(entries, rng, low, top_value):
    spot = [jax.random.randint(jax.random.fold_in(rng, axis), (), 0, length) for axis, length in enumerate(entries.shape)]
    main_axis = entries.shape.index(max(entries.shape))
    beside = spot[:main_axis] + [(spot[main_axis] + 1) % entries.shape[main_axis]] + spot[main_axis + 1:]
    return entries.at[tuple(spot)].set(low).at[tuple(beside)].set(top_value)


def block_scale(rng, shape, cuts, low, high):
    loudness, own = 1.0, jax.random.fold_in(rng, 6)
    for axis_at, blocks in cuts:
        steps = jnp.exp(jax.random.uniform(jax.random.fold_in(own, axis_at), (blocks,), jnp.float32, low / len(cuts), high / len(cuts)))
        loudness = loudness * jnp.repeat(steps, shape[axis_at] // blocks).reshape([-1 if axis == axis_at else 1 for axis in range(len(shape))])
    return loudness


def assign_block(rng, own, number, rows, number_of, top, bound, lean):
    order = jax.random.permutation(rng, number_of)
    packed, usual = shares(number_of, rows * top, bound, lean, True), shares(number_of, rows * top, bound, lean, False)
    places = jnp.arange(number_of)

    def named(lengths, rotation):
        used = int((lengths > 0).sum())
        fixed = max(1, used // 4)
        passed = fixed + (places - fixed + rotation * (used - fixed)) % max(1, number_of - fixed)
        return jnp.zeros((number_of,), jnp.int32).at[order[jnp.where(places < fixed, places, passed)]].set(jnp.asarray(lengths, jnp.int32))

    lengths = jnp.where(number % 4 == 0, named(packed, number // 4), named(usual, number - number // 4 - 1))
    mixed = jax.random.permutation(jax.random.fold_in(own, 3), number_of)
    donor, taker = mixed[0:number_of // 2 * 2:2], mixed[1:number_of // 2 * 2:2]
    margin = jnp.minimum(lengths[donor] - 1, bound - lengths[taker]) // 2
    margin = jnp.where((donor == order[0]) | (taker == order[0]) | (lengths[taker] == 0), 0, jnp.maximum(margin, 0))
    passed = jax.random.randint(jax.random.fold_in(own, 4), (number_of // 2,), 0, 1 << 20) % (margin + 1)
    lengths = lengths.at[donor].add(-passed).at[taker].add(passed)
    labels = jnp.searchsorted(jnp.cumsum(lengths), jnp.arange(rows * top), side="right").astype(jnp.int32)
    listing = labels.reshape(top, rows).T
    listing = listing[jax.random.permutation(jax.random.fold_in(own, 1), rows)]
    rotation = jax.random.randint(jax.random.fold_in(own, 2), (rows, 1), 0, top)
    return jnp.take_along_axis(listing, (jnp.arange(top)[None, :] + rotation) % top, axis=1)


def shares(number_of, total, limit, lean, full):
    weights = [(1 << 20) // math.isqrt(rank ** lean) + 1 for rank in range(1, number_of + 1)]
    largest = limit if full else min(limit, max(-(-total // number_of), total * weights[0] // sum(weights)))
    least = 1 if total - largest >= number_of - 1 else 0
    given, spare = [largest] + [least] * (number_of - 1), total - largest - least * (number_of - 1)
    while spare > 0:
        free = [i for i in range(1, number_of) if given[i] < largest] or [i for i in range(1, number_of) if given[i] < limit]
        pool, budget = sum([weights[i] for i in free]), spare
        for i in free:
            more = min(limit - given[i], max(1, budget * weights[i] // pool), spare)
            given[i] = given[i] + more
            spare = spare - more
    return np.array(given)


def scatter_about(key, dims, spread, reach, cuts=(), kind=jnp.bfloat16):
    entries = spread * jax.random.normal(key, dims, jnp.float32)
    if cuts:
        entries = entries * block_scale(key, dims, cuts, -0.22, 0.18)
    return jnp.clip(entries, -reach, reach).astype(kind)


def setup_inputs(seed: int = 0) -> dict:
    key_of = jax.random.split(jax.random.key(seed), 19)
    tokens = scatter_about(key_of[0], (NSEQ, LEN, D), 1.0, 6.0, ((0, 16), (1, 2)))
    norm_gain = jnp.clip(1.0 + 0.1 * jax.random.normal(key_of[1], (D,), jnp.float32), 0.5, 1.5).astype(jnp.bfloat16)
    query_proj = scatter_about(key_of[2], (D, H * (DN + DR)), D ** -0.5, 0.125, ((0, 32),))
    latent_proj = scatter_about(key_of[3], (D, KVL + DR), D ** -0.5, 0.125, ((0, 32),))
    latent_gain = jnp.clip(1.0 + 0.1 * jax.random.normal(key_of[4], (KVL,), jnp.float32), 0.5, 1.5).astype(jnp.bfloat16)
    expand_proj = scatter_about(key_of[5], (KVL, H * (DN + DV)), KVL ** -0.5, 0.25, ((0, 32),))
    output_proj = scatter_about(key_of[6], (H * DV, D), (H * DV // 16) ** -0.5, 0.5, ((0, 32),))
    mixer_gain = jnp.clip(1.0 + 0.1 * jax.random.normal(key_of[7], (D,), jnp.float32), 0.5, 1.5).astype(jnp.bfloat16)
    shared_gate = scatter_about(key_of[8], (D, SFF), D ** -0.5, 0.125, ((0, 32),))
    shared_up = scatter_about(key_of[9], (D, SFF), D ** -0.5, 0.125, ((0, 32),))
    shared_down = scatter_about(key_of[10], (SFF, D), (SFF // 2) ** -0.5, 0.15625, ((0, 32),))
    expert_gate = scatter_about(key_of[11], (EXPERTS, D, FF), D ** -0.5, 0.125, ((0, 16), (2, 2)))
    expert_up = scatter_about(key_of[12], (EXPERTS, D, FF), D ** -0.5, 0.125, ((0, 16), (2, 2)))
    expert_down = scatter_about(key_of[13], (EXPERTS, FF, D), (FF // 8) ** -0.5, 0.4375, ((0, 16), (1, 2)))
    doc_starts = draw_doc_starts(jax.random.fold_in(key_of[18], 71), 0)
    routes_keys = jax.random.split(jax.random.fold_in(key_of[15], 1), NSEQ * LEN // TOK_DEV)
    routes_turns = jax.random.permutation(jax.random.fold_in(key_of[15], 3), NSEQ * LEN // TOK_DEV)
    routes = jax.vmap(lambda own, number: assign_block(jax.random.fold_in(key_of[15], 2), own, number, TOK_DEV, EXPERTS, TOPK, CAP, 1))(routes_keys, routes_turns).reshape((NSEQ, LEN, TOPK))
    gate_levels = set_ends(jax.random.randint(key_of[16], (NSEQ, LEN, TOPK), 1, 9), jax.random.fold_in(key_of[16], 1), 1, 8).astype(jnp.int32)
    cotangent = scatter_about(key_of[17], (NSEQ, LEN, D), 1.0, 6.0, ((0, 16), (1, 2)))
    return {"tokens": tokens, "norm_gain": norm_gain, "query_proj": query_proj, "latent_proj": latent_proj, "latent_gain": latent_gain, "expand_proj": expand_proj, "output_proj": output_proj, "mixer_gain": mixer_gain, "shared_gate": shared_gate, "shared_up": shared_up, "shared_down": shared_down, "expert_gate": expert_gate, "expert_up": expert_up, "expert_down": expert_down, "doc_starts": doc_starts, "routes": routes, "gate_levels": gate_levels, "cotangent": cotangent}


norm_epsilon = 1e-06
rotary_base = 10000.0

@jax.custom_vjp
def low(v):
    return lax.optimization_barrier(v.astype(jnp.bfloat16)).astype(jnp.float32)

@jax.custom_vjp
def low_back(v):
    return v

def low_keep(v):
    return (low(v), None)

def low_pass(kept, grad):
    return (grad,)

def back_keep(v):
    return (v, None)

def back_low(kept, grad):
    return (low(grad),)
low.defvjp(low_keep, low_pass)
low_back.defvjp(back_keep, back_low)

def product(left, right):
    return jnp.dot(left, right, precision=lax.Precision.HIGHEST, preferred_element_type=jnp.float32)

def norm_apply(values, gain):
    inverse = lax.rsqrt(lax.optimization_barrier(jnp.mean(values * values, axis=-1, keepdims=True)) + norm_epsilon)
    return values * inverse * gain

def sigmoid_linear(values):
    return values * jax.nn.sigmoid(values)

def rotary_tables(positions, width):
    halfway = width // 2
    frequency = rotary_base ** (-2.0 * jnp.arange(halfway, dtype=jnp.float32) / width)
    angles = positions.astype(jnp.float32)[:, None] * frequency[None, :]
    return (jnp.cos(angles), jnp.sin(angles))

def rotate(values, cosine, sine):
    halfway = values.shape[-1] // 2
    leading = values[..., :halfway]
    trailing = values[..., halfway:]
    return jnp.concatenate([leading * cosine - trailing * sine, leading * sine + trailing * cosine], axis=-1)

def attend(pieces):
    query, keys, values, documents = pieces
    spots = jnp.arange(documents.shape[0])
    allowed = (spots[None, :] <= spots[:, None]) & (documents[None, :] == documents[:, None])
    scores = jnp.einsum('qhd,khd->hqk', query, keys, precision=lax.Precision.HIGHEST) * (DN + DR) ** (-0.5)
    scores = low_back(scores)
    scores = jnp.where(allowed[None], scores, -1e+30)
    peak_value = lax.optimization_barrier(jnp.max(scores, axis=-1, keepdims=True))
    expanded = jnp.exp(scores - peak_value)
    soft = expanded / lax.optimization_barrier(jnp.sum(expanded, axis=-1, keepdims=True))
    mixed = jnp.einsum('hqk,khd->qhd', low(soft), values, precision=lax.Precision.HIGHEST)
    return low_back(low(mixed))

def route_experts(normed_two, expert_gate, expert_up, expert_down, routes, gate_levels):
    chosen = routes.reshape(-1).astype(jnp.int32)
    pair_count = chosen.shape[0]
    matches = (chosen[:, None] == jnp.arange(EXPERTS, dtype=jnp.int32)[None, :]).astype(jnp.int32)
    loads = lax.optimization_barrier(jnp.sum(matches, axis=0))
    offsets = jnp.cumsum(loads) - loads
    ordering = jnp.argsort(chosen, stable=True).astype(jnp.int32)
    per_expert = CAP * N_SEQ * N_FSDP
    columns = jnp.arange(per_expert, dtype=jnp.int32)
    wanted = jnp.minimum(offsets[:, None] + columns[None, :], pair_count - 1).astype(jnp.int32)
    present = columns[None, :] < loads[:, None]
    picked = ordering[wanted]
    levels = gate_levels.reshape(-1, TOPK).astype(jnp.float32)
    gate_share = (levels / lax.optimization_barrier(jnp.sum(levels, axis=1, keepdims=True))).reshape(-1)
    weights = jnp.where(present, gate_share[picked], 0.0)
    sources = (picked // TOPK).astype(jnp.int32)

    def expert_apply(pieces):
        source_rows, gate_weight, up_weight, down_weight = pieces
        taken = low_back(jnp.take(normed_two, source_rows, axis=0))
        hidden = low(sigmoid_linear(low_back(product(taken, gate_weight))) * low_back(product(taken, up_weight)))
        return low(low_back(product(hidden, down_weight)))
    outputs = lax.map(jax.checkpoint(expert_apply), (sources, expert_gate, expert_up, expert_down))
    contributions = (weights[:, :, None] * outputs).reshape(-1, D)
    return jnp.zeros_like(normed_two).at[sources.reshape(-1)].add(contributions)

def forward(tokens, norm_gain, query_proj, latent_proj, latent_gain, expand_proj, output_proj, mixer_gain, shared_gate, shared_up, shared_down, expert_gate, expert_up, expert_down, documents, routes, gate_levels):
    total_rows = NSEQ * LEN
    inputs = tokens.reshape(total_rows, D)
    normed = low(norm_apply(inputs, norm_gain))
    query_raw = low_back(product(normed, query_proj)).reshape(total_rows, H, DN + DR)
    latent_raw = low_back(product(normed, latent_proj))
    latent_normed = low(norm_apply(latent_raw[:, :KVL], latent_gain))
    expanded = product(latent_normed, expand_proj).reshape(total_rows, H, DN + DV)
    positions = jnp.tile(jnp.arange(LEN, dtype=jnp.int32), NSEQ)
    cosine, sine = rotary_tables(positions, DR)
    query = low_back(low(jnp.concatenate([query_raw[:, :, :DN], rotate(query_raw[:, :, DN:], cosine[:, None, :], sine[:, None, :])], axis=2)))
    key_rotary = rotate(latent_raw[:, KVL:], cosine, sine)
    keys = low_back(low(jnp.concatenate([expanded[:, :, :DN], jnp.broadcast_to(key_rotary[:, None, :], (total_rows, H, DR))], axis=2)))
    values = low_back(low(expanded[:, :, DN:]))
    mixed = lax.map(jax.checkpoint(attend), (query.reshape(NSEQ, LEN, H, DN + DR), keys.reshape(NSEQ, LEN, H, DN + DR), values.reshape(NSEQ, LEN, H, DV), documents))
    attended = mixed.reshape(total_rows, H * DV)
    middle = inputs + low_back(product(attended, output_proj))
    normed_two = low(norm_apply(middle, mixer_gain))
    shared_hidden = low(sigmoid_linear(low_back(product(normed_two, shared_gate))) * low_back(product(normed_two, shared_up)))
    shared_result = low_back(product(shared_hidden, shared_down))
    routed = route_experts(normed_two, expert_gate, expert_up, expert_down, routes, gate_levels)
    return middle + shared_result + routed

def reference(tokens, norm_gain, query_proj, latent_proj, latent_gain, expand_proj, output_proj, mixer_gain, shared_gate, shared_up, shared_down, expert_gate, expert_up, expert_down, doc_starts, routes, gate_levels, cotangent):
    documents = jnp.cumsum(doc_starts, axis=1).astype(jnp.float32)
    floats = [argument.astype(jnp.float32) for argument in (tokens, norm_gain, query_proj, latent_proj, latent_gain, expand_proj, output_proj, mixer_gain, shared_gate, shared_up, shared_down, expert_gate, expert_up, expert_down)]

    def apply(*arrays):
        return forward(*arrays, documents, routes, gate_levels)
    output, pullback = jax.vjp(apply, *floats)
    gradients = pullback(cotangent.astype(jnp.float32).reshape(NSEQ * LEN, D))
    return (output.reshape(NSEQ, LEN, D), gradients[0], gradients[1], gradients[2], gradients[3], gradients[4], gradients[5], gradients[6], gradients[7], gradients[8], gradients[9], gradients[10], gradients[11], gradients[12], gradients[13])
```

```python
import functools

import jax
import jax.numpy as jnp
from jax import lax
from jax.experimental import pallas as pl
from jax.experimental.pallas import tpu as pltpu
from jax.sharding import PartitionSpec as P


H = 16
DN = 128
DR = 64
DV = 128
KVL = 512
TOPK = 6


norm_epsilon = 1e-06
rotary_base = 10000.0


def norm_apply(values, gain):
    inverse = lax.rsqrt(jnp.mean(values * values, axis=-1, keepdims=True) + norm_epsilon)
    return values * inverse * gain


def sigmoid_linear(values):
    return values * jax.nn.sigmoid(values)


def rotary_tables(positions, width):
    halfway = width // 2
    frequency = rotary_base ** (-2.0 * jnp.arange(halfway, dtype=jnp.float32) / width)
    angles = positions.astype(jnp.float32)[:, None] * frequency[None, :]
    return (jnp.cos(angles), jnp.sin(angles))


def rotate(values, cosine, sine):
    halfway = values.shape[-1] // 2
    leading = values[..., :halfway]
    trailing = values[..., halfway:]
    return jnp.concatenate(
        [leading * cosine - trailing * sine, leading * sine + trailing * cosine], axis=-1
    )


def contract(left, right, left_dim, right_dim):
    return lax.dot_general(
        left, right, (((left_dim,), (right_dim,)), ((), ())), preferred_element_type=jnp.float32
    )


def silu_slope(values):
    sigma = jax.nn.sigmoid(values)
    return sigma * (1.0 + values * (1.0 - sigma))


def forward(params, tokens, doc_starts, routes, gate_levels):
    (
        norm_gain,
        query_proj,
        latent_proj,
        latent_gain,
        expand_proj,
        output_proj,
        mixer_gain,
        shared_gate,
        shared_up,
        shared_down,
        expert_gate,
        expert_up,
        expert_down,
    ) = params
    gathered = (
        lax.all_gather(norm_gain, ("seq", "fsdp"), axis=0, tiled=True),
        lax.all_gather(query_proj, ("seq", "fsdp"), axis=0, tiled=True),
        lax.all_gather(latent_proj, ("seq", "fsdp"), axis=0, tiled=True),
        lax.all_gather(latent_gain, ("seq", "fsdp"), axis=0, tiled=True),
        lax.all_gather(expand_proj, ("seq", "fsdp"), axis=0, tiled=True),
        lax.all_gather(output_proj, ("seq", "fsdp"), axis=0, tiled=True),
        lax.all_gather(mixer_gain, ("seq", "fsdp"), axis=0, tiled=True),
        lax.all_gather(shared_gate, ("seq", "fsdp"), axis=0, tiled=True),
        lax.all_gather(shared_up, ("seq", "fsdp"), axis=0, tiled=True),
        lax.all_gather(shared_down, ("seq", "fsdp"), axis=0, tiled=True),
    )
    inputs = tokens[0].astype(jnp.float32)
    tok_count = inputs.shape[0]
    normed = norm_apply(inputs, gathered[0].astype(jnp.float32)).astype(jnp.bfloat16)
    query_raw = jnp.dot(normed, gathered[1], preferred_element_type=jnp.float32).reshape(
        tok_count, H, DN + DR
    )
    latent_raw = jnp.dot(normed, gathered[2], preferred_element_type=jnp.float32)
    latent = latent_raw[:, :KVL]
    latent_normed = norm_apply(latent, gathered[3].astype(jnp.float32)).astype(jnp.bfloat16)
    expanded = jnp.dot(latent_normed, gathered[4], preferred_element_type=jnp.float32).reshape(
        tok_count, H, DN + DV
    )
    positions = lax.axis_index("seq") * tok_count + jnp.arange(tok_count, dtype=jnp.int32)
    cosine, sine = rotary_tables(positions, DR)
    query = jnp.concatenate(
        [query_raw[:, :, :DN], rotate(query_raw[:, :, DN:], cosine[:, None, :], sine[:, None, :])],
        axis=2,
    ).astype(jnp.bfloat16)
    key_rotary = rotate(latent_raw[:, KVL:], cosine, sine)
    keys = jnp.concatenate(
        [expanded[:, :, :DN], jnp.broadcast_to(key_rotary[:, None, :], (tok_count, H, DR))], axis=2
    ).astype(jnp.bfloat16)
    values = expanded[:, :, DN:].astype(jnp.bfloat16)
    head_query, head_keys, head_values = (
        lax.all_to_all(query, "seq", split_axis=1, concat_axis=0, tiled=True),
        lax.all_to_all(keys, "seq", split_axis=1, concat_axis=0, tiled=True),
        lax.all_to_all(values, "seq", split_axis=1, concat_axis=0, tiled=True),
    )
    documents = jnp.cumsum(doc_starts[0])
    spots = jnp.arange(documents.shape[0])
    allowed = (spots[None, :] <= spots[:, None]) & (documents[None, :] == documents[:, None])
    scores = jnp.einsum(
        "qhd,khd->hqk", head_query, head_keys, preferred_element_type=jnp.float32
    ) * (DN + DR) ** (-0.5)
    scores = jnp.where(allowed[None], scores, -1e30)
    raised = jnp.exp(scores - jnp.max(scores, axis=-1, keepdims=True))
    soft = raised / jnp.sum(raised, axis=-1, keepdims=True)
    soft_low = soft.astype(jnp.bfloat16)
    mixed = jnp.einsum(
        "hqk,khd->qhd", soft_low, head_values, preferred_element_type=jnp.float32
    ).astype(jnp.bfloat16)
    returned = lax.all_to_all(mixed, "seq", split_axis=0, concat_axis=1, tiled=True)
    attended = returned.reshape(tok_count, H * DV)
    middle = inputs + jnp.dot(attended, gathered[5], preferred_element_type=jnp.float32)
    normed_two = norm_apply(middle, gathered[6].astype(jnp.float32)).astype(jnp.bfloat16)
    shared_pre = jnp.dot(normed_two, gathered[7], preferred_element_type=jnp.float32)
    shared_lift = jnp.dot(normed_two, gathered[8], preferred_element_type=jnp.float32)
    shared_hidden = (sigmoid_linear(shared_pre) * shared_lift).astype(jnp.bfloat16)
    shared_result = jnp.dot(shared_hidden, gathered[9], preferred_element_type=jnp.float32)
    experts_count = lax.axis_size("fsdp")
    capacity = max(2, 3 * tok_count * TOPK // (2 * experts_count))
    chosen = routes[0].reshape(-1)
    matches = (chosen[:, None] == jnp.arange(experts_count, dtype=jnp.int32)[None, :]).astype(
        jnp.int32
    )
    earlier = jnp.sum((jnp.cumsum(matches, axis=0) - matches) * matches, axis=1)
    slots = chosen * capacity + earlier
    filled = (
        jnp.zeros((experts_count * capacity,), jnp.int32)
        .at[slots]
        .set(jnp.arange(chosen.shape[0], dtype=jnp.int32) + 1)
    )
    present = filled > 0
    sources = jnp.maximum(filled - 1, 0)
    outgoing = jnp.where(
        present[:, None], jnp.take(normed_two, sources // TOPK, axis=0), jnp.zeros((), jnp.bfloat16)
    )
    arrived = lax.all_to_all(
        outgoing.reshape(experts_count, capacity, -1),
        "fsdp",
        split_axis=0,
        concat_axis=0,
        tiled=True,
    )
    paired = lax.all_gather(arrived, "seq", axis=0, tiled=True)
    expert_rows = paired.reshape(-1, paired.shape[-1])
    gate_weight, up_weight, down_weight = (expert_gate[0], expert_up[0], expert_down[0])
    expert_pre = jnp.dot(expert_rows, gate_weight, preferred_element_type=jnp.float32)
    expert_lift = jnp.dot(expert_rows, up_weight, preferred_element_type=jnp.float32)
    expert_hidden = (sigmoid_linear(expert_pre) * expert_lift).astype(jnp.bfloat16)
    partial_out = jnp.dot(expert_hidden, down_weight, preferred_element_type=jnp.float32)
    summed = lax.psum_scatter(
        partial_out.reshape(paired.shape).astype(jnp.bfloat16),
        "seq",
        scatter_dimension=0,
        tiled=True,
    )
    results = lax.all_to_all(summed, "fsdp", split_axis=0, concat_axis=0, tiled=True)
    picked = jnp.take(results.reshape(experts_count * capacity, -1), slots, axis=0)
    picked = picked.astype(jnp.float32).reshape(tok_count, TOPK, -1)
    levels = gate_levels[0].astype(jnp.float32)
    gate_share = levels / jnp.sum(levels, axis=1, keepdims=True)
    routed = jnp.sum(gate_share[:, :, None] * picked, axis=1)
    output = middle + shared_result + routed
    return dict(
        gathered=gathered,
        inputs=inputs,
        normed=normed,
        latent=latent,
        latent_normed=latent_normed,
        cosine=cosine,
        sine=sine,
        head_query=head_query,
        head_keys=head_keys,
        head_values=head_values,
        soft=soft,
        soft_low=soft_low,
        attended=attended,
        middle=middle,
        normed_two=normed_two,
        shared_pre=shared_pre,
        shared_lift=shared_lift,
        shared_hidden=shared_hidden,
        capacity=capacity,
        slots=slots,
        present=present,
        sources=sources,
        expert_rows=expert_rows,
        expert_pre=expert_pre,
        expert_lift=expert_lift,
        expert_hidden=expert_hidden,
        expert_weights=(gate_weight, up_weight, down_weight),
        gate_share=gate_share,
        output=output,
    )


def backward(saved, cotangent):
    gate_weight, up_weight, down_weight = saved["expert_weights"]
    gathered = saved["gathered"]
    grad_out = cotangent[0].astype(jnp.float32)
    grad_low = cotangent[0]
    tok_count = grad_out.shape[0]
    experts_count = lax.axis_size("fsdp")
    capacity = saved["capacity"]
    d_picked = (saved["gate_share"][:, :, None] * grad_out[:, None, :]).astype(jnp.bfloat16)
    d_picked = d_picked.reshape(tok_count * TOPK, -1)
    d_slots = jnp.where(
        saved["present"][:, None],
        jnp.take(d_picked, saved["sources"], axis=0),
        jnp.zeros((), jnp.bfloat16),
    )
    d_arrived = lax.all_to_all(
        d_slots.reshape(experts_count, capacity, -1),
        "fsdp",
        split_axis=0,
        concat_axis=0,
        tiled=True,
    )
    d_paired = lax.all_gather(d_arrived, "seq", axis=0, tiled=True)
    d_expert_out = d_paired.reshape(-1, d_paired.shape[-1])
    expert_pre = saved["expert_pre"]
    expert_rows = saved["expert_rows"]
    expert_down_grad = contract(saved["expert_hidden"], d_expert_out, 0, 0)
    d_hidden = contract(d_expert_out, down_weight, 1, 1)
    d_pre = (d_hidden * saved["expert_lift"] * silu_slope(expert_pre)).astype(jnp.bfloat16)
    d_lift = (d_hidden * sigmoid_linear(expert_pre)).astype(jnp.bfloat16)
    expert_gate_grad = contract(expert_rows, d_pre, 0, 0)
    expert_up_grad = contract(expert_rows, d_lift, 0, 0)
    d_rows = contract(d_pre, gate_weight, 1, 1) + contract(d_lift, up_weight, 1, 1)
    d_summed = lax.psum_scatter(
        d_rows.reshape(d_paired.shape).astype(jnp.bfloat16), "seq", scatter_dimension=0, tiled=True
    )
    d_back = lax.all_to_all(d_summed, "fsdp", split_axis=0, concat_axis=0, tiled=True)
    d_routed = jnp.take(d_back.reshape(experts_count * capacity, -1), saved["slots"], axis=0)
    d_routed = jnp.sum(d_routed.astype(jnp.float32).reshape(tok_count, TOPK, -1), axis=1)
    shared_pre = saved["shared_pre"]
    normed_two = saved["normed_two"]
    shared_down_grad = contract(saved["shared_hidden"], grad_low, 0, 0)
    d_shared_hidden = contract(grad_low, gathered[9], 1, 1)
    d_shared_pre = (d_shared_hidden * saved["shared_lift"] * silu_slope(shared_pre)).astype(
        jnp.bfloat16
    )
    d_shared_lift = (d_shared_hidden * sigmoid_linear(shared_pre)).astype(jnp.bfloat16)
    shared_gate_grad = contract(normed_two, d_shared_pre, 0, 0)
    shared_up_grad = contract(normed_two, d_shared_lift, 0, 0)
    d_normed_two = (
        contract(d_shared_pre, gathered[7], 1, 1)
        + contract(d_shared_lift, gathered[8], 1, 1)
        + d_routed
    )
    mixer_value, mixer_pull = jax.vjp(norm_apply, saved["middle"], gathered[6].astype(jnp.float32))
    d_middle_norm, mixer_gain_grad = mixer_pull(d_normed_two)
    d_middle = grad_out + d_middle_norm
    d_attn = d_middle.astype(jnp.bfloat16)
    output_proj_grad = contract(saved["attended"], d_attn, 0, 0)
    d_attended = contract(d_attn, gathered[5], 1, 1).astype(jnp.bfloat16).reshape(tok_count, H, DV)
    d_mixed = lax.all_to_all(d_attended, "seq", split_axis=1, concat_axis=0, tiled=True)
    soft = saved["soft"]
    d_soft = jnp.einsum(
        "qhd,khd->hqk", d_mixed, saved["head_values"], preferred_element_type=jnp.float32
    )
    delta = jnp.sum(soft * d_soft, axis=-1, keepdims=True)
    d_scores = (soft * (d_soft - delta)).astype(jnp.bfloat16)
    score_scale = (DN + DR) ** (-0.5)
    d_head_values = jnp.einsum(
        "hqk,qhd->khd", saved["soft_low"], d_mixed, preferred_element_type=jnp.float32
    ).astype(jnp.bfloat16)
    d_head_query = (
        jnp.einsum("hqk,khd->qhd", d_scores, saved["head_keys"], preferred_element_type=jnp.float32)
        * score_scale
    ).astype(jnp.bfloat16)
    d_head_keys = (
        jnp.einsum(
            "hqk,qhd->khd", d_scores, saved["head_query"], preferred_element_type=jnp.float32
        )
        * score_scale
    ).astype(jnp.bfloat16)
    d_query, d_keys, d_values = (
        lax.all_to_all(d_head_query, "seq", split_axis=0, concat_axis=1, tiled=True),
        lax.all_to_all(d_head_keys, "seq", split_axis=0, concat_axis=1, tiled=True),
        lax.all_to_all(d_head_values, "seq", split_axis=0, concat_axis=1, tiled=True),
    )
    cosine = saved["cosine"]
    sine = saved["sine"]
    normed = saved["normed"]
    d_query_float = d_query.astype(jnp.float32)
    d_query_raw = (
        jnp.concatenate(
            [
                d_query_float[:, :, :DN],
                rotate(d_query_float[:, :, DN:], cosine[:, None, :], -sine[:, None, :]),
            ],
            axis=2,
        )
        .astype(jnp.bfloat16)
        .reshape(tok_count, -1)
    )
    query_proj_grad = contract(normed, d_query_raw, 0, 0)
    d_key_rotary = rotate(jnp.sum(d_keys[:, :, DN:].astype(jnp.float32), axis=1), cosine, -sine)
    d_expanded = jnp.concatenate([d_keys[:, :, :DN], d_values], axis=2).reshape(tok_count, -1)
    expand_proj_grad = contract(saved["latent_normed"], d_expanded, 0, 0)
    d_latent_normed = contract(d_expanded, gathered[4], 1, 1)
    latent_value, latent_pull = jax.vjp(
        norm_apply, saved["latent"], gathered[3].astype(jnp.float32)
    )
    d_latent, latent_gain_grad = latent_pull(d_latent_normed)
    d_latent_raw = jnp.concatenate([d_latent, d_key_rotary], axis=1).astype(jnp.bfloat16)
    latent_proj_grad = contract(normed, d_latent_raw, 0, 0)
    d_normed = contract(d_query_raw, gathered[1], 1, 1) + contract(d_latent_raw, gathered[2], 1, 1)
    input_value, input_pull = jax.vjp(norm_apply, saved["inputs"], gathered[0].astype(jnp.float32))
    d_inputs, norm_gain_grad = input_pull(d_normed)
    input_grad = d_middle + d_inputs
    reduced = (
        lax.psum_scatter(norm_gain_grad, ("seq", "fsdp"), scatter_dimension=0, tiled=True),
        lax.psum_scatter(query_proj_grad, ("seq", "fsdp"), scatter_dimension=0, tiled=True),
        lax.psum_scatter(latent_proj_grad, ("seq", "fsdp"), scatter_dimension=0, tiled=True),
        lax.psum_scatter(latent_gain_grad, ("seq", "fsdp"), scatter_dimension=0, tiled=True),
        lax.psum_scatter(expand_proj_grad, ("seq", "fsdp"), scatter_dimension=0, tiled=True),
        lax.psum_scatter(output_proj_grad, ("seq", "fsdp"), scatter_dimension=0, tiled=True),
        lax.psum_scatter(mixer_gain_grad, ("seq", "fsdp"), scatter_dimension=0, tiled=True),
        lax.psum_scatter(shared_gate_grad, ("seq", "fsdp"), scatter_dimension=0, tiled=True),
        lax.psum_scatter(shared_up_grad, ("seq", "fsdp"), scatter_dimension=0, tiled=True),
        lax.psum_scatter(shared_down_grad, ("seq", "fsdp"), scatter_dimension=0, tiled=True),
    )
    return (input_grad, reduced, expert_gate_grad, expert_up_grad, expert_down_grad)


def copy_rows(dst, src, rows):
    def body(i, carry):
        r = pl.multiple_of(i * 16, 16)
        dst[pl.ds(r, 16), :] = src[pl.ds(r, 16), :]
        return carry

    lax.fori_loop(0, rows // 16, body, 0)


def gather_all(block, cid):
    return lax.all_gather(block, ("seq", "fsdp"), axis=0, tiled=False)


def scatter_sum(parts, cid):
    total = lax.psum_scatter(parts, ("seq", "fsdp"), scatter_dimension=0, tiled=False)
    return total.astype(jnp.float32)


def spread_all(blocks, cid):
    return lax.all_to_all(blocks, ("seq", "fsdp"), split_axis=0, concat_axis=0, tiled=True)


def seq_swap(pieces, cid):
    seq = lax.axis_index("seq")
    mine = lax.dynamic_index_in_dim(pieces, seq, axis=0, keepdims=False)
    other = lax.dynamic_index_in_dim(pieces, 1 - seq, axis=0, keepdims=False)
    return jnp.stack([mine, lax.ppermute(other, "seq", [(0, 1), (1, 0)])])


def pass_kernel(x_ref, o_ref):
    copy_rows(o_ref, x_ref, x_ref.shape[0])


def pass_on(block):
    return pl.pallas_call(
        pass_kernel, out_shape=jax.ShapeDtypeStruct(block.shape, block.dtype), name="pass_on"
    )(block)


def norm_back(values, gain, upstream):
    value, pull = jax.vjp(norm_apply, values, gain)
    return pull(upstream)


def block_body(
    tokens,
    norm_gain,
    query_proj,
    latent_proj,
    latent_gain,
    expand_proj,
    output_proj,
    mixer_gain,
    shared_gate,
    shared_up,
    shared_down,
    expert_gate,
    expert_up,
    expert_down,
    doc_starts,
    routes,
    gate_levels,
    cotangent,
):
    bf, f32 = jnp.bfloat16, jnp.float32
    seq = lax.axis_index("seq")
    fsdp = lax.axis_index("fsdp")
    both = ("seq", "fsdp")
    inputs = tokens[0].astype(f32)
    toks, width = inputs.shape
    n_dev = 32
    rows = query_proj.shape[0]
    latent_rows = expand_proj.shape[0]
    groups = rows // latent_rows
    n_q, n_o, n_l = query_proj.shape[1], output_proj.shape[1], latent_proj.shape[1]
    n_e = expand_proj.shape[1] // groups
    experts_count = 16
    capacity = 3 * toks * TOPK // (2 * experts_count)

    chosen = routes[0]
    levels = gate_levels[0]
    by_expert = jnp.sum(
        jnp.where(
            chosen.T[:, None, :] == jnp.arange(experts_count, dtype=jnp.int32)[None, :, None],
            levels.T[:, None, :],
            0,
        ),
        axis=0,
    )
    info = jnp.concatenate([by_expert, jnp.sum(levels, axis=1)[None]], axis=0).astype(bf)
    info = jnp.pad(info, ((0, rows - info.shape[0]), (0, 0)))
    folded = jnp.concatenate(jnp.split(expand_proj, groups, axis=1), axis=0)
    gains = jnp.stack([norm_gain, mixer_gain, jnp.pad(latent_gain, (0, rows - latent_rows))], axis=1)
    gains = jnp.pad(gains, ((0, 0), (0, 64 - 3)))
    packed = jnp.concatenate([query_proj, output_proj, latent_proj, gains, folded, info], axis=1)
    spots = [0]
    for part in (n_q, n_o, n_l, 64, n_e, toks):
        spots.append(spots[-1] + part)
    weights = gather_all(packed, 1)
    w_query = weights[:, :, : spots[1]].reshape(width, n_q)
    w_output = weights[:, :, spots[1] : spots[2]].reshape(width, n_o)
    w_latent = weights[:, :, spots[2] : spots[3]].reshape(width, n_l)
    all_gains = weights[:, :, spots[3] : spots[4]].astype(f32)
    gain_one = all_gains[:, :, 0].reshape(-1)
    gain_two = all_gains[:, :, 1].reshape(-1)
    gain_latent = all_gains[:, :latent_rows, 2].reshape(-1)
    w_expand = weights[:, :, spots[4] : spots[5]].reshape(n_dev, groups, latent_rows, n_e)
    w_expand = jnp.swapaxes(w_expand, 1, 2).reshape(KVL, groups * n_e)
    all_info = weights[:, :, spots[5] :].astype(f32)

    n_s = shared_down.shape[0]
    fill = jnp.zeros((rows, n_dev, 256 - 2 * n_s), bf)
    gate_up = jnp.concatenate(
        [shared_gate.reshape(rows, n_dev, n_s), shared_up.reshape(rows, n_dev, n_s), fill], axis=2
    )
    w_shared = spread_all(jnp.swapaxes(gate_up, 0, 1), 11).reshape(width, -1)[:, : 2 * n_s]

    cot_all = gather_all(cotangent[0], 3).reshape(-1, width)

    normed = norm_apply(inputs, gain_one).astype(bf)
    query_raw = jnp.dot(normed, w_query, preferred_element_type=f32).reshape(toks, H, DN + DR)
    latent_raw = jnp.dot(normed, w_latent, preferred_element_type=f32)
    latent = latent_raw[:, :KVL]
    latent_normed = norm_apply(latent, gain_latent).astype(bf)
    positions = seq * toks + jnp.arange(toks, dtype=jnp.int32)
    cosine, sine = rotary_tables(positions, DR)
    query = jnp.concatenate(
        [query_raw[:, :, :DN], rotate(query_raw[:, :, DN:], cosine[:, None, :], sine[:, None, :])],
        axis=2,
    ).astype(bf)
    key_rotary = rotate(latent_raw[:, KVL:], cosine, sine).astype(bf)
    own = jnp.concatenate([latent_normed, key_rotary, jnp.zeros((toks, 64), bf)], axis=1)
    pair = seq_swap(jnp.stack([own, own]), 4)
    pair = jnp.where(seq == 0, pair, pair[::-1]).reshape(2 * toks, -1)
    latent_full = pair[:, :KVL]
    rotary_full = pair[:, KVL : KVL + DR]
    expanded = jnp.dot(latent_full, w_expand, preferred_element_type=f32).astype(bf)
    expanded = expanded.reshape(2 * toks, H, DN + DV)
    keys, values = expanded[:, :, :DN], expanded[:, :, DN:]
    keys = jnp.concatenate(
        [keys, jnp.broadcast_to(rotary_full[:, None, :], (2 * toks, H, DR))], axis=2
    )
    documents = jnp.cumsum(doc_starts[0])
    key_spots = jnp.arange(2 * toks)
    own_documents = lax.dynamic_slice(documents, (seq * toks,), (toks,))
    allowed = (key_spots[None, :] <= positions[:, None]) & (
        documents[None, :] == own_documents[:, None]
    )
    score_scale = (DN + DR) ** (-0.5)
    scores = jnp.einsum("qhd,khd->hqk", query, keys, preferred_element_type=f32) * score_scale
    scores = jnp.where(allowed[None], scores, -1e30)
    raised = jnp.exp(scores - jnp.max(scores, axis=-1, keepdims=True))
    soft = raised / jnp.sum(raised, axis=-1, keepdims=True)
    soft_low = soft.astype(bf)
    mixed = jnp.einsum("hqk,khd->qhd", soft_low, values, preferred_element_type=f32).astype(bf)
    attended = mixed.reshape(toks, H * DV)
    middle = inputs + jnp.dot(attended, w_output, preferred_element_type=f32)
    normed_two = pass_on(norm_apply(middle, gain_two).astype(bf))

    gathered = gather_all(normed_two, 5)
    x_all = gathered.reshape(-1, width)
    level = lax.dynamic_index_in_dim(all_info, fsdp, axis=1, keepdims=False)
    mask = level > 0
    share = level / all_info[:, experts_count]
    slot = jnp.cumsum(mask.astype(jnp.int32), axis=1) - 1
    pick = mask[:, None, :] & (
        slot[:, None, :] == jnp.arange(capacity, dtype=jnp.int32)[None, :, None]
    )
    share_rows = jnp.sum(jnp.where(pick, share[:, None, :], 0.0), axis=2)
    pick = pick.astype(bf)
    expert_rows = jnp.einsum("bst,btd->bsd", pick, gathered, preferred_element_type=f32)
    expert_rows = expert_rows.astype(bf).reshape(n_dev * capacity, width)
    gate_weight, up_weight, down_weight = expert_gate[0], expert_up[0], expert_down[0]
    n_h = gate_weight.shape[1]
    expert_pre = jnp.dot(expert_rows, gate_weight, preferred_element_type=f32)
    expert_lift = jnp.dot(expert_rows, up_weight, preferred_element_type=f32)
    expert_hidden = (sigmoid_linear(expert_pre) * expert_lift).astype(bf)
    shared_both = jnp.dot(x_all, w_shared, preferred_element_type=f32)
    shared_pre, shared_lift = shared_both[:, :n_s], shared_both[:, n_s:]
    shared_hidden = (sigmoid_linear(shared_pre) * shared_lift).astype(bf)
    spread = jnp.einsum(
        "bst,bsd->btd",
        pick,
        expert_hidden.reshape(n_dev, capacity, n_h),
        preferred_element_type=f32,
    )
    spread = (spread * share[:, :, None]).astype(bf).reshape(-1, n_h)
    hidden_all = jnp.concatenate([spread, shared_hidden], axis=1)
    down_all = jnp.concatenate([down_weight, shared_down], axis=0)
    out_parts = jnp.dot(hidden_all, down_all, preferred_element_type=f32).astype(bf)
    layer_out = middle + scatter_sum(out_parts.reshape(n_dev, toks, width), 6)

    grad_out = cotangent[0].astype(f32)
    d_rows = jnp.einsum(
        "bst,btd->bsd", pick, cot_all.reshape(n_dev, toks, width), preferred_element_type=f32
    )
    d_rows = (d_rows * share_rows[:, :, None]).astype(bf).reshape(n_dev * capacity, width)
    expert_down_grad = contract(expert_hidden, d_rows, 0, 0)
    d_hidden = contract(d_rows, down_weight, 1, 1)
    d_pre = (d_hidden * expert_lift * silu_slope(expert_pre)).astype(bf)
    d_lift = (d_hidden * sigmoid_linear(expert_pre)).astype(bf)
    expert_gate_grad = contract(expert_rows, d_pre, 0, 0)
    expert_up_grad = contract(expert_rows, d_lift, 0, 0)
    d_x = contract(d_pre, gate_weight, 1, 1) + contract(d_lift, up_weight, 1, 1)
    d_x = d_x.astype(bf).reshape(n_dev, capacity, width)
    d_x = jnp.einsum("bst,bsd->btd", pick, d_x, preferred_element_type=f32).reshape(-1, width)
    shared_down_grad = contract(shared_hidden, cot_all, 0, 0)
    d_shared_hidden = contract(cot_all, shared_down, 1, 1)
    d_shared_pre = (d_shared_hidden * shared_lift * silu_slope(shared_pre)).astype(bf)
    d_shared_lift = (d_shared_hidden * sigmoid_linear(shared_pre)).astype(bf)
    d_shared_both = jnp.concatenate([d_shared_pre, d_shared_lift], axis=1)
    shared_both_grad = contract(x_all, d_shared_both, 0, 0).astype(bf)
    d_x = (d_x + contract(d_shared_both, w_shared, 1, 1)).astype(bf)
    d_normed_two = scatter_sum(d_x.reshape(n_dev, toks, width), 7)
    shared_both_grad = jnp.pad(shared_both_grad, ((0, 0), (0, 256 - 2 * n_s)))
    shared_back = spread_all(shared_both_grad.reshape(n_dev, rows, 256), 12)
    shared_back = jnp.swapaxes(shared_back, 0, 1).astype(f32)
    shared_gate_grad = shared_back[:, :, :n_s].reshape(rows, n_dev * n_s)
    shared_up_grad = shared_back[:, :, n_s : 2 * n_s].reshape(rows, n_dev * n_s)

    d_middle_norm, mixer_gain_grad = norm_back(middle, gain_two, d_normed_two)
    d_middle = grad_out + d_middle_norm
    d_attn = d_middle.astype(bf)
    output_proj_grad = contract(attended, d_attn, 0, 0)
    d_mixed = contract(d_attn, w_output, 1, 1).astype(bf).reshape(toks, H, DV)
    d_soft = jnp.einsum("qhd,khd->hqk", d_mixed, values, preferred_element_type=f32)
    delta = jnp.sum(soft * d_soft, axis=-1, keepdims=True)
    d_scores = (soft * (d_soft - delta)).astype(bf)
    d_values = jnp.einsum("hqk,qhd->khd", soft_low, d_mixed, preferred_element_type=f32).astype(bf)
    d_query = (
        jnp.einsum("hqk,khd->qhd", d_scores, keys, preferred_element_type=f32) * score_scale
    )
    d_keys = (
        jnp.einsum("hqk,qhd->khd", d_scores, query, preferred_element_type=f32) * score_scale
    )
    d_query_raw = (
        jnp.concatenate(
            [
                d_query[:, :, :DN],
                rotate(d_query[:, :, DN:], cosine[:, None, :], -sine[:, None, :]),
            ],
            axis=2,
        )
        .astype(bf)
        .reshape(toks, -1)
    )
    query_proj_grad = contract(normed, d_query_raw, 0, 0)
    d_expanded = jnp.concatenate([d_keys[:, :, :DN].astype(bf), d_values], axis=2)
    d_expanded = d_expanded.reshape(2 * toks, -1)
    expand_proj_grad = contract(latent_full, d_expanded, 0, 0)
    d_latent_pair = contract(d_expanded, w_expand, 1, 1)
    d_rotary_pair = jnp.sum(d_keys[:, :, DN:], axis=1)
    d_pair = jnp.concatenate(
        [d_latent_pair, d_rotary_pair, jnp.zeros((2 * toks, 64), f32)], axis=1
    ).reshape(2, toks, -1)
    d_pair = jnp.sum(seq_swap(d_pair, 8), axis=0)
    d_latent_normed = d_pair[:, :KVL]
    d_key_rotary = rotate(d_pair[:, KVL : KVL + DR], cosine, -sine)
    d_latent, latent_gain_grad = norm_back(latent, gain_latent, d_latent_normed)
    d_latent_raw = jnp.concatenate([d_latent, d_key_rotary], axis=1).astype(bf)
    latent_proj_grad = contract(normed, d_latent_raw, 0, 0)
    d_normed = contract(d_query_raw, w_query, 1, 1) + contract(d_latent_raw, w_latent, 1, 1)
    d_inputs, norm_gain_grad = norm_back(inputs, gain_one, d_normed)
    input_grad = d_middle + d_inputs

    folded_grad = expand_proj_grad.astype(bf).reshape(n_dev, latent_rows, groups, n_e)
    folded_grad = jnp.swapaxes(folded_grad, 1, 2).reshape(n_dev, rows, n_e)
    latent_gain_part = jnp.pad(
        latent_gain_grad.reshape(n_dev, latent_rows), ((0, 0), (0, rows - latent_rows))
    )
    gain_parts = jnp.stack(
        [
            norm_gain_grad.reshape(n_dev, rows),
            mixer_gain_grad.reshape(n_dev, rows),
            latent_gain_part,
        ],
        axis=2,
    )
    gain_parts = jnp.pad(gain_parts, ((0, 0), (0, 0), (0, 64 - 3))).astype(bf)
    out_parts_grad = output_proj_grad.astype(bf).reshape(n_dev, rows, n_o)
    output_grad = scatter_sum(out_parts_grad, 9)
    grad_parts = jnp.concatenate(
        [
            query_proj_grad.astype(bf).reshape(n_dev, rows, n_q),
            folded_grad,
            latent_proj_grad.astype(bf).reshape(n_dev, rows, n_l),
            gain_parts,
        ],
        axis=2,
    )
    grads = scatter_sum(grad_parts, 10)
    at_latent = n_q + n_e
    at_gain = at_latent + n_l
    expand_out = jnp.concatenate(
        jnp.split(grads[:, n_q:at_latent], groups, axis=0), axis=1
    )
    return (
        layer_out[None],
        input_grad[None],
        grads[:, at_gain],
        grads[:, :n_q],
        grads[:, at_latent:at_gain],
        grads[:latent_rows, at_gain + 2],
        expand_out,
        output_grad,
        grads[:, at_gain + 1],
        shared_gate_grad,
        shared_up_grad,
        shared_down_grad,
        expert_gate_grad[None],
        expert_up_grad[None],
        expert_down_grad[None],
    )


def plain_body(
    tokens,
    norm_gain,
    query_proj,
    latent_proj,
    latent_gain,
    expand_proj,
    output_proj,
    mixer_gain,
    shared_gate,
    shared_up,
    shared_down,
    expert_gate,
    expert_up,
    expert_down,
    doc_starts,
    routes,
    gate_levels,
    cotangent,
):
    params = (
        norm_gain,
        query_proj,
        latent_proj,
        latent_gain,
        expand_proj,
        output_proj,
        mixer_gain,
        shared_gate,
        shared_up,
        shared_down,
        expert_gate,
        expert_up,
        expert_down,
    )
    saved = forward(params, tokens, doc_starts, routes, gate_levels)
    layer_out = saved["output"]
    input_grad, reduced, expert_gate_grad, expert_up_grad, expert_down_grad = backward(
        saved, cotangent
    )
    return (
        layer_out[None],
        input_grad[None],
        reduced[0],
        reduced[1],
        reduced[2],
        reduced[3],
        reduced[4],
        reduced[5],
        reduced[6],
        reduced[7],
        reduced[8],
        reduced[9],
        expert_gate_grad[None],
        expert_up_grad[None],
        expert_down_grad[None],
    )


def solution(mesh):
    in_specs = (
        P("fsdp", "seq", None),
        P(("seq", "fsdp")),
        P(("seq", "fsdp"), None),
        P(("seq", "fsdp"), None),
        P(("seq", "fsdp")),
        P(("seq", "fsdp"), None),
        P(("seq", "fsdp"), None),
        P(("seq", "fsdp")),
        P(("seq", "fsdp"), None),
        P(("seq", "fsdp"), None),
        P(("seq", "fsdp"), None),
        P("fsdp", None, "seq"),
        P("fsdp", None, "seq"),
        P("fsdp", "seq", None),
        P("fsdp", None),
        P("fsdp", "seq", None),
        P("fsdp", "seq", None),
        P("fsdp", "seq", None),
    )
    out_specs = (
        P("fsdp", "seq", None),
        P("fsdp", "seq", None),
        P(("seq", "fsdp")),
        P(("seq", "fsdp"), None),
        P(("seq", "fsdp"), None),
        P(("seq", "fsdp")),
        P(("seq", "fsdp"), None),
        P(("seq", "fsdp"), None),
        P(("seq", "fsdp")),
        P(("seq", "fsdp"), None),
        P(("seq", "fsdp"), None),
        P(("seq", "fsdp"), None),
        P("fsdp", None, "seq"),
        P("fsdp", None, "seq"),
        P("fsdp", "seq", None),
    )
    chosen = block_body if dict(mesh.shape) == {"seq": 2, "fsdp": 16} else plain_body
    return jax.shard_map(chosen, mesh=mesh, in_specs=in_specs, out_specs=out_specs, check_vma=False)
```

```python
import functools

import jax
import jax.numpy as jnp
from jax import lax
from jax.experimental import pallas as pl
from jax.experimental.pallas import tpu as pltpu
from jax.sharding import PartitionSpec as P


H = 16
DN = 128
DR = 64
DV = 128
KVL = 512
TOPK = 6


norm_epsilon = 1e-06
rotary_base = 10000.0


def norm_apply(values, gain):
    inverse = lax.rsqrt(jnp.mean(values * values, axis=-1, keepdims=True) + norm_epsilon)
    return values * inverse * gain


def sigmoid_linear(values):
    return values * jax.nn.sigmoid(values)


def rotary_tables(positions, width):
    halfway = width // 2
    frequency = rotary_base ** (-2.0 * jnp.arange(halfway, dtype=jnp.float32) / width)
    angles = positions.astype(jnp.float32)[:, None] * frequency[None, :]
    return (jnp.cos(angles), jnp.sin(angles))


def rotate(values, cosine, sine):
    halfway = values.shape[-1] // 2
    leading = values[..., :halfway]
    trailing = values[..., halfway:]
    return jnp.concatenate(
        [leading * cosine - trailing * sine, leading * sine + trailing * cosine], axis=-1
    )


def contract(left, right, left_dim, right_dim):
    return lax.dot_general(
        left, right, (((left_dim,), (right_dim,)), ((), ())), preferred_element_type=jnp.float32
    )


def silu_slope(values):
    sigma = jax.nn.sigmoid(values)
    return sigma * (1.0 + values * (1.0 - sigma))


def forward(params, tokens, doc_starts, routes, gate_levels):
    (
        norm_gain,
        query_proj,
        latent_proj,
        latent_gain,
        expand_proj,
        output_proj,
        mixer_gain,
        shared_gate,
        shared_up,
        shared_down,
        expert_gate,
        expert_up,
        expert_down,
    ) = params
    gathered = (
        lax.all_gather(norm_gain, ("seq", "fsdp"), axis=0, tiled=True),
        lax.all_gather(query_proj, ("seq", "fsdp"), axis=0, tiled=True),
        lax.all_gather(latent_proj, ("seq", "fsdp"), axis=0, tiled=True),
        lax.all_gather(latent_gain, ("seq", "fsdp"), axis=0, tiled=True),
        lax.all_gather(expand_proj, ("seq", "fsdp"), axis=0, tiled=True),
        lax.all_gather(output_proj, ("seq", "fsdp"), axis=0, tiled=True),
        lax.all_gather(mixer_gain, ("seq", "fsdp"), axis=0, tiled=True),
        lax.all_gather(shared_gate, ("seq", "fsdp"), axis=0, tiled=True),
        lax.all_gather(shared_up, ("seq", "fsdp"), axis=0, tiled=True),
        lax.all_gather(shared_down, ("seq", "fsdp"), axis=0, tiled=True),
    )
    inputs = tokens[0].astype(jnp.float32)
    tok_count = inputs.shape[0]
    normed = norm_apply(inputs, gathered[0].astype(jnp.float32)).astype(jnp.bfloat16)
    query_raw = jnp.dot(normed, gathered[1], preferred_element_type=jnp.float32).reshape(
        tok_count, H, DN + DR
    )
    latent_raw = jnp.dot(normed, gathered[2], preferred_element_type=jnp.float32)
    latent = latent_raw[:, :KVL]
    latent_normed = norm_apply(latent, gathered[3].astype(jnp.float32)).astype(jnp.bfloat16)
    expanded = jnp.dot(latent_normed, gathered[4], preferred_element_type=jnp.float32).reshape(
        tok_count, H, DN + DV
    )
    positions = lax.axis_index("seq") * tok_count + jnp.arange(tok_count, dtype=jnp.int32)
    cosine, sine = rotary_tables(positions, DR)
    query = jnp.concatenate(
        [query_raw[:, :, :DN], rotate(query_raw[:, :, DN:], cosine[:, None, :], sine[:, None, :])],
        axis=2,
    ).astype(jnp.bfloat16)
    key_rotary = rotate(latent_raw[:, KVL:], cosine, sine)
    keys = jnp.concatenate(
        [expanded[:, :, :DN], jnp.broadcast_to(key_rotary[:, None, :], (tok_count, H, DR))], axis=2
    ).astype(jnp.bfloat16)
    values = expanded[:, :, DN:].astype(jnp.bfloat16)
    head_query, head_keys, head_values = (
        lax.all_to_all(query, "seq", split_axis=1, concat_axis=0, tiled=True),
        lax.all_to_all(keys, "seq", split_axis=1, concat_axis=0, tiled=True),
        lax.all_to_all(values, "seq", split_axis=1, concat_axis=0, tiled=True),
    )
    documents = jnp.cumsum(doc_starts[0])
    spots = jnp.arange(documents.shape[0])
    allowed = (spots[None, :] <= spots[:, None]) & (documents[None, :] == documents[:, None])
    scores = jnp.einsum(
        "qhd,khd->hqk", head_query, head_keys, preferred_element_type=jnp.float32
    ) * (DN + DR) ** (-0.5)
    scores = jnp.where(allowed[None], scores, -1e30)
    raised = jnp.exp(scores - jnp.max(scores, axis=-1, keepdims=True))
    soft = raised / jnp.sum(raised, axis=-1, keepdims=True)
    soft_low = soft.astype(jnp.bfloat16)
    mixed = jnp.einsum(
        "hqk,khd->qhd", soft_low, head_values, preferred_element_type=jnp.float32
    ).astype(jnp.bfloat16)
    returned = lax.all_to_all(mixed, "seq", split_axis=0, concat_axis=1, tiled=True)
    attended = returned.reshape(tok_count, H * DV)
    middle = inputs + jnp.dot(attended, gathered[5], preferred_element_type=jnp.float32)
    normed_two = norm_apply(middle, gathered[6].astype(jnp.float32)).astype(jnp.bfloat16)
    shared_pre = jnp.dot(normed_two, gathered[7], preferred_element_type=jnp.float32)
    shared_lift = jnp.dot(normed_two, gathered[8], preferred_element_type=jnp.float32)
    shared_hidden = (sigmoid_linear(shared_pre) * shared_lift).astype(jnp.bfloat16)
    shared_result = jnp.dot(shared_hidden, gathered[9], preferred_element_type=jnp.float32)
    experts_count = lax.axis_size("fsdp")
    capacity = max(2, 3 * tok_count * TOPK // (2 * experts_count))
    chosen = routes[0].reshape(-1)
    matches = (chosen[:, None] == jnp.arange(experts_count, dtype=jnp.int32)[None, :]).astype(
        jnp.int32
    )
    earlier = jnp.sum((jnp.cumsum(matches, axis=0) - matches) * matches, axis=1)
    slots = chosen * capacity + earlier
    filled = (
        jnp.zeros((experts_count * capacity,), jnp.int32)
        .at[slots]
        .set(jnp.arange(chosen.shape[0], dtype=jnp.int32) + 1)
    )
    present = filled > 0
    sources = jnp.maximum(filled - 1, 0)
    outgoing = jnp.where(
        present[:, None], jnp.take(normed_two, sources // TOPK, axis=0), jnp.zeros((), jnp.bfloat16)
    )
    arrived = lax.all_to_all(
        outgoing.reshape(experts_count, capacity, -1),
        "fsdp",
        split_axis=0,
        concat_axis=0,
        tiled=True,
    )
    paired = lax.all_gather(arrived, "seq", axis=0, tiled=True)
    expert_rows = paired.reshape(-1, paired.shape[-1])
    gate_weight, up_weight, down_weight = (expert_gate[0], expert_up[0], expert_down[0])
    expert_pre = jnp.dot(expert_rows, gate_weight, preferred_element_type=jnp.float32)
    expert_lift = jnp.dot(expert_rows, up_weight, preferred_element_type=jnp.float32)
    expert_hidden = (sigmoid_linear(expert_pre) * expert_lift).astype(jnp.bfloat16)
    partial_out = jnp.dot(expert_hidden, down_weight, preferred_element_type=jnp.float32)
    summed = lax.psum_scatter(
        partial_out.reshape(paired.shape).astype(jnp.bfloat16),
        "seq",
        scatter_dimension=0,
        tiled=True,
    )
    results = lax.all_to_all(summed, "fsdp", split_axis=0, concat_axis=0, tiled=True)
    picked = jnp.take(results.reshape(experts_count * capacity, -1), slots, axis=0)
    picked = picked.astype(jnp.float32).reshape(tok_count, TOPK, -1)
    levels = gate_levels[0].astype(jnp.float32)
    gate_share = levels / jnp.sum(levels, axis=1, keepdims=True)
    routed = jnp.sum(gate_share[:, :, None] * picked, axis=1)
    output = middle + shared_result + routed
    return dict(
        gathered=gathered,
        inputs=inputs,
        normed=normed,
        latent=latent,
        latent_normed=latent_normed,
        cosine=cosine,
        sine=sine,
        head_query=head_query,
        head_keys=head_keys,
        head_values=head_values,
        soft=soft,
        soft_low=soft_low,
        attended=attended,
        middle=middle,
        normed_two=normed_two,
        shared_pre=shared_pre,
        shared_lift=shared_lift,
        shared_hidden=shared_hidden,
        capacity=capacity,
        slots=slots,
        present=present,
        sources=sources,
        expert_rows=expert_rows,
        expert_pre=expert_pre,
        expert_lift=expert_lift,
        expert_hidden=expert_hidden,
        expert_weights=(gate_weight, up_weight, down_weight),
        gate_share=gate_share,
        output=output,
    )


def backward(saved, cotangent):
    gate_weight, up_weight, down_weight = saved["expert_weights"]
    gathered = saved["gathered"]
    grad_out = cotangent[0].astype(jnp.float32)
    grad_low = cotangent[0]
    tok_count = grad_out.shape[0]
    experts_count = lax.axis_size("fsdp")
    capacity = saved["capacity"]
    d_picked = (saved["gate_share"][:, :, None] * grad_out[:, None, :]).astype(jnp.bfloat16)
    d_picked = d_picked.reshape(tok_count * TOPK, -1)
    d_slots = jnp.where(
        saved["present"][:, None],
        jnp.take(d_picked, saved["sources"], axis=0),
        jnp.zeros((), jnp.bfloat16),
    )
    d_arrived = lax.all_to_all(
        d_slots.reshape(experts_count, capacity, -1),
        "fsdp",
        split_axis=0,
        concat_axis=0,
        tiled=True,
    )
    d_paired = lax.all_gather(d_arrived, "seq", axis=0, tiled=True)
    d_expert_out = d_paired.reshape(-1, d_paired.shape[-1])
    expert_pre = saved["expert_pre"]
    expert_rows = saved["expert_rows"]
    expert_down_grad = contract(saved["expert_hidden"], d_expert_out, 0, 0)
    d_hidden = contract(d_expert_out, down_weight, 1, 1)
    d_pre = (d_hidden * saved["expert_lift"] * silu_slope(expert_pre)).astype(jnp.bfloat16)
    d_lift = (d_hidden * sigmoid_linear(expert_pre)).astype(jnp.bfloat16)
    expert_gate_grad = contract(expert_rows, d_pre, 0, 0)
    expert_up_grad = contract(expert_rows, d_lift, 0, 0)
    d_rows = contract(d_pre, gate_weight, 1, 1) + contract(d_lift, up_weight, 1, 1)
    d_summed = lax.psum_scatter(
        d_rows.reshape(d_paired.shape).astype(jnp.bfloat16), "seq", scatter_dimension=0, tiled=True
    )
    d_back = lax.all_to_all(d_summed, "fsdp", split_axis=0, concat_axis=0, tiled=True)
    d_routed = jnp.take(d_back.reshape(experts_count * capacity, -1), saved["slots"], axis=0)
    d_routed = jnp.sum(d_routed.astype(jnp.float32).reshape(tok_count, TOPK, -1), axis=1)
    shared_pre = saved["shared_pre"]
    normed_two = saved["normed_two"]
    shared_down_grad = contract(saved["shared_hidden"], grad_low, 0, 0)
    d_shared_hidden = contract(grad_low, gathered[9], 1, 1)
    d_shared_pre = (d_shared_hidden * saved["shared_lift"] * silu_slope(shared_pre)).astype(
        jnp.bfloat16
    )
    d_shared_lift = (d_shared_hidden * sigmoid_linear(shared_pre)).astype(jnp.bfloat16)
    shared_gate_grad = contract(normed_two, d_shared_pre, 0, 0)
    shared_up_grad = contract(normed_two, d_shared_lift, 0, 0)
    d_normed_two = (
        contract(d_shared_pre, gathered[7], 1, 1)
        + contract(d_shared_lift, gathered[8], 1, 1)
        + d_routed
    )
    mixer_value, mixer_pull = jax.vjp(norm_apply, saved["middle"], gathered[6].astype(jnp.float32))
    d_middle_norm, mixer_gain_grad = mixer_pull(d_normed_two)
    d_middle = grad_out + d_middle_norm
    d_attn = d_middle.astype(jnp.bfloat16)
    output_proj_grad = contract(saved["attended"], d_attn, 0, 0)
    d_attended = contract(d_attn, gathered[5], 1, 1).astype(jnp.bfloat16).reshape(tok_count, H, DV)
    d_mixed = lax.all_to_all(d_attended, "seq", split_axis=1, concat_axis=0, tiled=True)
    soft = saved["soft"]
    d_soft = jnp.einsum(
        "qhd,khd->hqk", d_mixed, saved["head_values"], preferred_element_type=jnp.float32
    )
    delta = jnp.sum(soft * d_soft, axis=-1, keepdims=True)
    d_scores = (soft * (d_soft - delta)).astype(jnp.bfloat16)
    score_scale = (DN + DR) ** (-0.5)
    d_head_values = jnp.einsum(
        "hqk,qhd->khd", saved["soft_low"], d_mixed, preferred_element_type=jnp.float32
    ).astype(jnp.bfloat16)
    d_head_query = (
        jnp.einsum("hqk,khd->qhd", d_scores, saved["head_keys"], preferred_element_type=jnp.float32)
        * score_scale
    ).astype(jnp.bfloat16)
    d_head_keys = (
        jnp.einsum(
            "hqk,qhd->khd", d_scores, saved["head_query"], preferred_element_type=jnp.float32
        )
        * score_scale
    ).astype(jnp.bfloat16)
    d_query, d_keys, d_values = (
        lax.all_to_all(d_head_query, "seq", split_axis=0, concat_axis=1, tiled=True),
        lax.all_to_all(d_head_keys, "seq", split_axis=0, concat_axis=1, tiled=True),
        lax.all_to_all(d_head_values, "seq", split_axis=0, concat_axis=1, tiled=True),
    )
    cosine = saved["cosine"]
    sine = saved["sine"]
    normed = saved["normed"]
    d_query_float = d_query.astype(jnp.float32)
    d_query_raw = (
        jnp.concatenate(
            [
                d_query_float[:, :, :DN],
                rotate(d_query_float[:, :, DN:], cosine[:, None, :], -sine[:, None, :]),
            ],
            axis=2,
        )
        .astype(jnp.bfloat16)
        .reshape(tok_count, -1)
    )
    query_proj_grad = contract(normed, d_query_raw, 0, 0)
    d_key_rotary = rotate(jnp.sum(d_keys[:, :, DN:].astype(jnp.float32), axis=1), cosine, -sine)
    d_expanded = jnp.concatenate([d_keys[:, :, :DN], d_values], axis=2).reshape(tok_count, -1)
    expand_proj_grad = contract(saved["latent_normed"], d_expanded, 0, 0)
    d_latent_normed = contract(d_expanded, gathered[4], 1, 1)
    latent_value, latent_pull = jax.vjp(
        norm_apply, saved["latent"], gathered[3].astype(jnp.float32)
    )
    d_latent, latent_gain_grad = latent_pull(d_latent_normed)
    d_latent_raw = jnp.concatenate([d_latent, d_key_rotary], axis=1).astype(jnp.bfloat16)
    latent_proj_grad = contract(normed, d_latent_raw, 0, 0)
    d_normed = contract(d_query_raw, gathered[1], 1, 1) + contract(d_latent_raw, gathered[2], 1, 1)
    input_value, input_pull = jax.vjp(norm_apply, saved["inputs"], gathered[0].astype(jnp.float32))
    d_inputs, norm_gain_grad = input_pull(d_normed)
    input_grad = d_middle + d_inputs
    reduced = (
        lax.psum_scatter(norm_gain_grad, ("seq", "fsdp"), scatter_dimension=0, tiled=True),
        lax.psum_scatter(query_proj_grad, ("seq", "fsdp"), scatter_dimension=0, tiled=True),
        lax.psum_scatter(latent_proj_grad, ("seq", "fsdp"), scatter_dimension=0, tiled=True),
        lax.psum_scatter(latent_gain_grad, ("seq", "fsdp"), scatter_dimension=0, tiled=True),
        lax.psum_scatter(expand_proj_grad, ("seq", "fsdp"), scatter_dimension=0, tiled=True),
        lax.psum_scatter(output_proj_grad, ("seq", "fsdp"), scatter_dimension=0, tiled=True),
        lax.psum_scatter(mixer_gain_grad, ("seq", "fsdp"), scatter_dimension=0, tiled=True),
        lax.psum_scatter(shared_gate_grad, ("seq", "fsdp"), scatter_dimension=0, tiled=True),
        lax.psum_scatter(shared_up_grad, ("seq", "fsdp"), scatter_dimension=0, tiled=True),
        lax.psum_scatter(shared_down_grad, ("seq", "fsdp"), scatter_dimension=0, tiled=True),
    )
    return (input_grad, reduced, expert_gate_grad, expert_up_grad, expert_down_grad)


MESH = pl.DeviceIdType.MESH

def busy(micros):
    return pl.CostEstimate(flops=0, bytes_accessed=int(micros * 3.5e6), transcendentals=0)


def coords():
    seq = lax.axis_index("seq")
    fsdp = lax.axis_index("fsdp")
    return seq, lax.rem(fsdp // 2, 2), fsdp // 4, lax.rem(fsdp, 2)

def device(x, y, z, c):
    return (x, (z * 2 + y) * 2 + c)

def place(x, y, z, c):
    return x * 16 + z * 4 + y * 2 + c

def greet(x, y, z, c):
    bar = pltpu.get_barrier_semaphore()
    for dev in (device(1 - x, y, z, c), device(x, 1 - y, z, c), device(x, y, z, 1 - c)):
        pl.semaphore_signal(bar, inc=1, device_id=dev, device_id_type=MESH)
    @pl.when(z > 0)
    def _():
        pl.semaphore_signal(bar, inc=1, device_id=device(x, y, z - 1, c), device_id_type=MESH)
    @pl.when(z < 3)
    def _():
        pl.semaphore_signal(bar, inc=1, device_id=device(x, y, z + 1, c), device_id_type=MESH)
    pl.semaphore_wait(bar, jnp.where((z > 0) & (z < 3), 5, 4))

def remote(src, dst, ss, rs, dev):
    return pltpu.make_async_remote_copy(src_ref=src, dst_ref=dst, send_sem=ss, recv_sem=rs, device_id=dev, device_id_type=MESH)

def near_order(z):
    w = jnp.where
    first = w(z == 0, 1, w(z == 1, 0, w(z == 2, 1, 2)))
    second = w(z == 0, 2, w(z == 1, 2, w(z == 2, 3, 1)))
    third = w(z == 0, 3, w(z == 1, 3, 0))
    return (first, second, third)

def ag_kernel(half, x_ref, o_ref, zs, zr, xs, xr, ys, yr, das, dar, dbs, dbr, cs, cr, ls):
    x, y, z, c = coords()
    greet(x, y, z, c)
    xm, ym, cm = device(1 - x, y, z, c), device(x, 1 - y, z, c), device(x, y, z, 1 - c)
    lo, hi = pl.ds(0, half), pl.ds(half, half)
    me = o_ref.at[place(x, y, z, c)]
    order = (z,) + near_order(z)
    sends = []
    local = pltpu.make_async_copy(x_ref, me, ls)
    local.start()
    def up(src, zz, sem):
        return remote(src, o_ref.at[place(x, y, zz, c)], zs.at[sem], zr.at[zz], device(x, y, z + 1, c))
    def down(src, zz, sem):
        return remote(src, o_ref.at[place(x, y, zz, c)], zs.at[sem], zr.at[zz], device(x, y, z - 1, c))
    @pl.when(z < 3)
    def _():
        up(x_ref, z, 0).start()
    @pl.when(z > 0)
    def _():
        down(x_ref, z, 1).start()
    def blk(dx, dy, zz, cc=None):
        return o_ref.at[place(jnp.abs(x - dx), jnp.abs(y - dy), zz, c if cc is None else cc)]
    def xsend(j):
        b = x_ref if j == 0 else blk(0, 0, order[j])
        return remote(b, blk(0, 0, order[j]), xs.at[j], xr.at[j], xm)
    def ysend(j):
        b = x_ref if j == 0 else blk(0, 0, order[j])
        return remote(b, blk(0, 0, order[j]), ys.at[j], yr.at[j], ym)
    def xrecv(j):
        b = blk(1, 0, order[j])
        return remote(b, b, xs.at[j], xr.at[j], xm)
    def yrecv(j):
        b = blk(0, 1, order[j])
        return remote(b, b, ys.at[j], yr.at[j], ym)
    def dasend(j):
        b = blk(1, 0, order[j]).at[lo]
        return remote(b, b, das.at[j], dar.at[j], ym)
    def dbsend(j):
        b = blk(0, 1, order[j]).at[hi]
        return remote(b, b, dbs.at[j], dbr.at[j], xm)
    def darecv(j):
        b = blk(1, 1, order[j]).at[lo]
        return remote(b, b, das.at[j], dar.at[j], ym)
    def dbrecv(j):
        b = blk(1, 1, order[j]).at[hi]
        return remote(b, b, dbs.at[j], dbr.at[j], xm)
    def csend(j, q):
        dx, dy = q % 2, q // 2
        b = blk(dx, dy, order[j])
        src = x_ref if (j == 0 and q == 0) else b
        return remote(src, b, cs.at[j * 4 + q], cr.at[j * 4 + q], cm)
    def crecv(j, q):
        b = blk(q % 2, q // 2, order[j], 1 - c)
        return remote(b, b, cs.at[j * 4 + q], cr.at[j * 4 + q], cm)
    def second(j):
        xrecv(j).wait_recv()
        dasend(j).start()
        csend(j, 1).start()
        yrecv(j).wait_recv()
        dbsend(j).start()
        csend(j, 2).start()
    def third(j):
        darecv(j).wait_recv()
        dbrecv(j).wait_recv()
        csend(j, 3).start()
    xsend(0).start()
    ysend(0).start()
    csend(0, 0).start()
    for j in (1, 2, 3):
        zz = order[j]
        b = o_ref.at[place(x, y, zz, c)]
        remote(b, b, zs.at[0], zr.at[zz], cm).wait_recv()
        @pl.when((zz < z) & (z < 3))
        def _():
            up(b, zz, j + 1).start()
        @pl.when((zz > z) & (z > 0))
        def _():
            down(b, zz, j + 1).start()
        xsend(j).start()
        ysend(j).start()
        csend(j, 0).start()
        second(j - 1)
        if j > 1:
            third(j - 2)
    second(3)
    third(2)
    third(3)
    local.wait()
    @pl.when(z < 3)
    def _():
        up(x_ref, z, 0).wait_send()
    @pl.when(z > 0)
    def _():
        down(x_ref, z, 1).wait_send()
    for j in range(4):
        if j:
            zz = order[j]
            b = o_ref.at[place(x, y, zz, c)]
            @pl.when((zz < z) & (z < 3))
            def _():
                up(b, zz, j + 1).wait_send()
            @pl.when((zz > z) & (z > 0))
            def _():
                down(b, zz, j + 1).wait_send()
        xsend(j).wait_send()
        ysend(j).wait_send()
        dasend(j).wait_send()
        dbsend(j).wait_send()
        for q in range(4):
            csend(j, q).wait_send()
            crecv(j, q).wait_recv()

DMA = pltpu.SemaphoreType.DMA

def gather_all(block, cid):
    rows, cols = block.shape
    grouped = (rows // 8, 8, cols)
    out = pl.pallas_call(
        functools.partial(ag_kernel, rows // 16),
        out_shape=jax.ShapeDtypeStruct((32,) + grouped, block.dtype),
        in_specs=[pl.BlockSpec(memory_space=pl.ANY)],
        out_specs=pl.BlockSpec(memory_space=pl.ANY),
        scratch_shapes=[DMA((5,)), DMA((4,))] + [DMA((4,))] * 8 + [DMA((16,)), DMA((16,)), DMA],
        compiler_params=pltpu.CompilerParams(
            collective_id=cid, has_side_effects=True, vmem_limit_bytes=60 * 2**20
        ),
        cost_estimate=busy(20 + block.size * block.dtype.itemsize / 8e3 ),
        name="gather_rows",
    )(block.reshape(grouped))
    return out


def far_order(z):
    w = jnp.where
    first = w(z < 2, 3, 0)
    second = w(z == 0, 2, w(z == 1, 0, w(z == 2, 3, 1)))
    third = w(z == 0, 1, w(z == 1, 2, w(z == 2, 1, 2)))
    return (first, second, third, z)

def rs_kernel(half, p_ref, o_ref, acc, cl, lxa, lya2, lyb, lxb2, zl, ls, cs, cr, xas, xar, ya2s, ya2r, ybs, ybr, xb2s, xb2r, zs, zr):
    x, y, z, c = coords()
    greet(x, y, z, c)
    xm, ym, cm = device(1 - x, y, z, c), device(x, 1 - y, z, c), device(x, y, z, 1 - c)
    order = far_order(z)
    rows = 2 * half
    lo, hi = pl.ds(0, half), pl.ds(half, half)
    def add(dst, at, src, src_at, count):
        def body(i, carry):
            d = dst.at[pl.ds(at + 2 * i, 2)]
            s = src.at[pl.ds(src_at + 2 * i, 2)]
            d[...] = (d[...].astype(jnp.float32) + s[...].astype(jnp.float32)).astype(d.dtype)
            return carry
        lax.fori_loop(0, count // 2, body, 0)
    def blk(q, zz, cc):
        return p_ref.at[place(jnp.abs(x - q % 2), jnp.abs(y - q // 2), zz, cc)]
    def load(j, q):
        return pltpu.make_async_copy(blk(q, order[j], c), acc.at[j, q], ls.at[j * 4 + q])
    def csend(j, q):
        return remote(blk(q, order[j], 1 - c), cl.at[j, q], cs.at[j * 4 + q], cr.at[j * 4 + q], cm)
    def xa(j, i):
        return remote(acc.at[j, 1 + 2 * i, lo], lxa.at[j, i], xas.at[j, i], xar.at[j, i], xm)
    def yb(j, i):
        return remote(acc.at[j, 2 + i, hi], lyb.at[j, i], ybs.at[j, i], ybr.at[j, i], ym)
    def ya2(j):
        return remote(acc.at[j, 2, lo], lya2.at[j], ya2s.at[j], ya2r.at[j], ym)
    def xb2(j):
        return remote(acc.at[j, 1, hi], lxb2.at[j], xb2s.at[j], xb2r.at[j], xm)
    firsts = (1, 3, 2, 0)
    for j in range(4):
        for q in firsts:
            csend(j, q).start()
            load(j, q).start()
    def one(j):
        for q in firsts:
            load(j, q).wait()
            csend(j, q).wait_recv()
            add(acc.at[j, q], 0, cl.at[j, q], 0, rows)
            if q == 1:
                xa(j, 0).start()
            if q == 3:
                xa(j, 1).start()
                yb(j, 1).start()
            if q == 2:
                yb(j, 0).start()
    def two(j):
        xa(j, 1).wait_recv()
        add(acc.at[j, 2], 0, lxa.at[j, 1], 0, half)
        ya2(j).start()
        yb(j, 1).wait_recv()
        add(acc.at[j, 1], half, lyb.at[j, 1], 0, half)
        xb2(j).start()
        xa(j, 0).wait_recv()
        add(acc.at[j, 0], 0, lxa.at[j, 0], 0, half)
        yb(j, 0).wait_recv()
        add(acc.at[j, 0], half, lyb.at[j, 0], 0, half)
    def zin(slot):
        return remote(zl.at[slot], zl.at[slot], zs.at[0], zr.at[slot], cm)
    def zout_up(j):
        return remote(acc.at[j, 0], zl.at[order[j]], zs.at[j], zr.at[order[j]], device(x, y, z + 1, c))
    def zout_down(j):
        slot = jnp.where(order[j] == z - 1, 4, order[j])
        return remote(acc.at[j, 0], zl.at[slot], zs.at[j], zr.at[slot], device(x, y, z - 1, c))
    def three(j):
        ya2(j).wait_recv()
        add(acc.at[j, 0], 0, lya2.at[j], 0, half)
        xb2(j).wait_recv()
        add(acc.at[j, 0], half, lxb2.at[j], 0, half)
        zz = order[j]
        if j < 3:
            @pl.when(((zz > z) & (z > 0)) | ((zz < z) & (z < 3)))
            def _():
                zin(zz).wait_recv()
                add(acc.at[j, 0], 0, zl.at[zz], 0, rows)
            @pl.when(zz > z)
            def _():
                zout_up(j).start()
            @pl.when(zz < z)
            def _():
                zout_down(j).start()
        else:
            @pl.when(z > 0)
            def _():
                zin(z).wait_recv()
                add(acc.at[j, 0], 0, zl.at[z], 0, rows)
            @pl.when(z < 3)
            def _():
                zin(4).wait_recv()
                add(acc.at[j, 0], 0, zl.at[4], 0, rows)
            def body(i, carry):
                o_ref[pl.ds(2 * i, 2)] = acc[3, 0, pl.ds(2 * i, 2)].astype(o_ref.dtype)
                return carry
            lax.fori_loop(0, rows // 2, body, 0)
    one(0)
    one(1)
    two(0)
    one(2)
    three(0)
    two(1)
    one(3)
    three(1)
    two(2)
    three(2)
    two(3)
    three(3)
    for j in range(4):
        for q in range(4):
            csend(j, q).wait_send()
        for i in range(2):
            xa(j, i).wait_send()
            yb(j, i).wait_send()
        ya2(j).wait_send()
        xb2(j).wait_send()
        if j < 3:
            zz = order[j]
            @pl.when(zz > z)
            def _():
                zout_up(j).wait_send()
            @pl.when(zz < z)
            def _():
                zout_down(j).wait_send()

def scatter_sum(parts, cid):
    _, rows, cols = parts.shape
    bf = parts.dtype
    whole, half = (rows // 8, 8, cols), (rows // 16, 8, cols)
    out = pl.pallas_call(
        functools.partial(rs_kernel, rows // 16),
        out_shape=jax.ShapeDtypeStruct(whole, jnp.float32),
        in_specs=[pl.BlockSpec(memory_space=pl.ANY)],
        out_specs=pl.BlockSpec(memory_space=pltpu.VMEM),
        scratch_shapes=[
            pltpu.VMEM((4, 4) + whole, bf),
            pltpu.VMEM((4, 4) + whole, bf),
            pltpu.VMEM((4, 2) + half, bf),
            pltpu.VMEM((4,) + half, bf),
            pltpu.VMEM((4, 2) + half, bf),
            pltpu.VMEM((4,) + half, bf),
            pltpu.VMEM((5,) + whole, bf),
            DMA((16,)), DMA((16,)), DMA((16,)), DMA((4, 2)), DMA((4, 2)), DMA((4,)), DMA((4,)),
            DMA((4, 2)), DMA((4, 2)), DMA((4,)), DMA((4,)), DMA((3,)), DMA((5,)),
        ],
        compiler_params=pltpu.CompilerParams(
            collective_id=cid, has_side_effects=True, vmem_limit_bytes=60 * 2**20
        ),
        cost_estimate=busy(20 + rows * cols * bf.itemsize / 8e3),
        name="scatter_sum",
    )(parts.reshape((32,) + whole))
    return out.reshape(rows, cols)


def spread_kernel(x_ref, o_ref, ls, ss, rs):
    x, y, z, c = coords()
    me = place(x, y, z, c)
    n_dev = x_ref.shape[0]

    def far(k):
        kx, kz, ky, kc = k // 16, lax.rem(k // 4, 4), lax.rem(k // 2, 2), lax.rem(k, 2)
        return jnp.abs(x - kx), jnp.abs(y - ky), lax.rem(z + kz, 4), jnp.abs(c - kc)

    bar = pltpu.get_barrier_semaphore()

    def greet_one(k, carry):
        pl.semaphore_signal(bar, inc=1, device_id=device(*far(k)), device_id_type=MESH)
        return carry

    lax.fori_loop(1, n_dev, greet_one, 0)

    pl.semaphore_wait(bar, n_dev - 1)

    def send(k):
        to = far(k)
        return remote(x_ref.at[place(*to)], o_ref.at[me], ss.at[k], rs.at[k], device(*to))

    def start(k, carry):
        send(k).start()
        return carry

    lax.fori_loop(1, n_dev, start, 0)
    local = pltpu.make_async_copy(x_ref.at[me], o_ref.at[me], ls)
    local.start()
    local.wait()

    def finish(k, carry):
        send(k).wait()
        return carry

    lax.fori_loop(1, n_dev, finish, 0)


def spread_all(blocks, cid):
    count, rows, cols = blocks.shape
    grouped = (count, rows // 8, 8, cols)
    out = pl.pallas_call(
        spread_kernel,
        out_shape=jax.ShapeDtypeStruct(grouped, blocks.dtype),
        in_specs=[pl.BlockSpec(memory_space=pl.ANY)],
        out_specs=pl.BlockSpec(memory_space=pl.ANY),
        scratch_shapes=[DMA, DMA((32,)), DMA((32,))],
        compiler_params=pltpu.CompilerParams(
            collective_id=cid, has_side_effects=True, vmem_limit_bytes=60 * 2**20
        ),
        cost_estimate=busy(25),
        name="spread_all",
    )(blocks.reshape(grouped))
    return out.reshape(blocks.shape)


def swap_kernel(x_ref, o_ref, ls, ss, rs):
    x, y, z, c = coords()
    mate = device(1 - x, y, z, c)
    bar = pltpu.get_barrier_semaphore()
    pl.semaphore_signal(bar, inc=1, device_id=mate, device_id_type=MESH)
    pl.semaphore_wait(bar, 1)
    out = remote(x_ref.at[1 - x], o_ref.at[1], ss, rs, mate)
    out.start()
    local = pltpu.make_async_copy(x_ref.at[x], o_ref.at[0], ls)
    local.start()
    local.wait()
    out.wait()


def seq_swap(pieces, cid):
    count, rows, cols = pieces.shape
    grouped = (count, rows // 8, 8, cols)
    out = pl.pallas_call(
        swap_kernel,
        out_shape=jax.ShapeDtypeStruct(grouped, pieces.dtype),
        in_specs=[pl.BlockSpec(memory_space=pl.ANY)],
        out_specs=pl.BlockSpec(memory_space=pl.ANY),
        scratch_shapes=[DMA, DMA, DMA],
        compiler_params=pltpu.CompilerParams(
            collective_id=cid, has_side_effects=True, vmem_limit_bytes=60 * 2**20
        ),
        cost_estimate=busy(8),
        name="seq_swap",
    )(pieces.reshape(grouped))
    return out.reshape(pieces.shape)


def columns_kernel(x_ref, w_ref, o_ref):
    o_ref[...] = jnp.dot(x_ref[...], w_ref[...], preferred_element_type=jnp.float32)


def times_columns(rows_in, weights, first, count, tile):
    m, k = rows_in.shape
    return pl.pallas_call(
        columns_kernel,
        grid=(count,),
        out_shape=jax.ShapeDtypeStruct((m, count * tile), jnp.float32),
        in_specs=[
            pl.BlockSpec((m, k), lambda i: (0, 0)),
            pl.BlockSpec((k, tile), lambda i: (0, first + i)),
        ],
        out_specs=pl.BlockSpec((m, tile), lambda i: (0, i)),
        compiler_params=pltpu.CompilerParams(vmem_limit_bytes=48 * 2**20),
        name="times_columns",
    )(rows_in, weights)


def rows_kernel(x_ref, w_ref, o_ref):
    o_ref[...] = contract(x_ref[...], w_ref[...], 1, 1)


def times_rows(rows_in, weights, at, width, tile):
    m = rows_in.shape[0]
    k = weights.shape[0]
    return pl.pallas_call(
        rows_kernel,
        grid=(k // tile,),
        out_shape=jax.ShapeDtypeStruct((m, k), jnp.float32),
        in_specs=[
            pl.BlockSpec((m, width), lambda i: (0, 0)),
            pl.BlockSpec((tile, width), lambda i: (i, at)),
        ],
        out_specs=pl.BlockSpec((m, tile), lambda i: (0, i)),
        compiler_params=pltpu.CompilerParams(vmem_limit_bytes=48 * 2**20),
        name="times_rows",
    )(rows_in, weights)


def expand_kernel(x_ref, w_ref, o_ref):
    weight = w_ref[...].reshape(x_ref.shape[1], w_ref.shape[2])
    o_ref[...] = jnp.dot(x_ref[...], weight, preferred_element_type=jnp.float32).astype(o_ref.dtype)


def times_folded(rows_in, weights, fold, at, width):
    m, k = rows_in.shape
    groups = weights.shape[1] // fold
    return pl.pallas_call(
        expand_kernel,
        grid=(groups,),
        out_shape=jax.ShapeDtypeStruct((m, groups * width), jnp.bfloat16),
        in_specs=[
            pl.BlockSpec((m, k), lambda g: (0, 0)),
            pl.BlockSpec((weights.shape[0], fold, width), lambda g: (0, g, at)),
        ],
        out_specs=pl.BlockSpec((m, width), lambda g: (0, g)),
        compiler_params=pltpu.CompilerParams(vmem_limit_bytes=48 * 2**20),
        name="times_folded",
    )(rows_in, weights)


def expand_back_kernel(x_ref, w_ref, o_ref):
    weight = w_ref[...].reshape(o_ref.shape[1], w_ref.shape[2])

    @pl.when(pl.program_id(0) == 0)
    def _():
        o_ref[...] = jnp.zeros_like(o_ref)

    o_ref[...] += contract(x_ref[...], weight, 1, 1)


def times_folded_back(rows_in, weights, fold, at, width):
    m = rows_in.shape[0]
    k = weights.shape[0] * fold
    groups = weights.shape[1] // fold
    return pl.pallas_call(
        expand_back_kernel,
        grid=(groups,),
        out_shape=jax.ShapeDtypeStruct((m, k), jnp.float32),
        in_specs=[
            pl.BlockSpec((m, width), lambda g: (0, g)),
            pl.BlockSpec((weights.shape[0], fold, width), lambda g: (0, g, at)),
        ],
        out_specs=pl.BlockSpec((m, k), lambda g: (0, 0)),
        compiler_params=pltpu.CompilerParams(vmem_limit_bytes=48 * 2**20),
        name="times_folded_back",
    )(rows_in, weights)


def grads_kernel(
    tile, n_q, n_e, n_o, fold, normed_ref, dq_ref, full_ref, dexp_ref, att_ref, dattn_ref, dlat_ref, gain_ref, o_ref
):
    t = pl.program_id(0)
    n_dev, rows, _ = o_ref.shape
    t_q, t_e, t_o = n_q // tile, n_e // tile, n_o // tile

    def cut(ref, i):
        return ref[:, pl.ds(pl.multiple_of(i * tile, tile), tile)]

    def put(left, right):
        done = jnp.dot(left, right, preferred_element_type=jnp.float32).astype(o_ref.dtype)
        return done.reshape(n_dev, done.shape[0] // n_dev, tile)

    @pl.when(t < t_q)
    def _():
        o_ref[...] = put(normed_ref[...], cut(dq_ref, t))

    @pl.when((t >= t_q) & (t < t_q + t_e))
    def _():
        for g in range(rows // fold):
            part = cut(dexp_ref, g * t_e + t - t_q)
            o_ref[:, g * fold : (g + 1) * fold, :] = put(full_ref[...], part)

    @pl.when((t >= t_q + t_e) & (t < t_q + t_e + t_o))
    def _():
        o_ref[...] = put(att_ref[...], cut(dattn_ref, t - t_q - t_e))

    @pl.when(t >= t_q + t_e + t_o)
    def _():
        i = t - t_q - t_e - t_o
        o_ref[...] = put(normed_ref[...], cut(dlat_ref, i)) + cut_gain(gain_ref, i, tile)


def cut_gain(ref, i, tile):
    return ref[:, :, pl.ds(pl.multiple_of(i * tile, tile), tile)]


def packed_grads(n_dev, rows, fold, normed, dq, full, dexp, att, dattn, dlat, gain):
    tile = 256
    n_q, n_e, n_o, n_l = dq.shape[1], dexp.shape[1] // (rows // fold), dattn.shape[1], dlat.shape[1]
    cols = n_q + n_e + n_o + n_l
    whole = lambda a: pl.BlockSpec(a.shape, lambda i: (0,) * a.ndim)
    operands = (normed, dq, full, dexp, att, dattn, dlat, gain)
    return pl.pallas_call(
        functools.partial(grads_kernel, tile, n_q, n_e, n_o, fold),
        grid=(cols // tile,),
        out_shape=jax.ShapeDtypeStruct((n_dev, rows, cols), jnp.bfloat16),
        in_specs=[whole(a) for a in operands],
        out_specs=pl.BlockSpec((n_dev, rows, tile), lambda i: (0, 0, i)),
        compiler_params=pltpu.CompilerParams(vmem_limit_bytes=56 * 2**20),
        name="packed_grads",
    )(*operands)


def picks(pick_ref, share_ref):
    pairs, slots, toks = pick_ref.shape
    found = []
    for p in range(pairs):
        pick = pick_ref[p]
        scale = jnp.sum(pick.astype(jnp.float32) * share_ref[p], axis=1, keepdims=True)
        r, t = slice(p * slots, (p + 1) * slots), slice(p * toks, (p + 1) * toks)
        found.append((pick, r, t, scale))
    return found


def forward_kernel(
    x_ref, pick_ref, share_ref, wg_ref, wu_ref, wd_ref, ws_ref, wsd_ref,
    out_ref, rows_ref, pre_ref, lift_ref, hid_ref, both_ref, hs_ref,
):
    f32, bf = jnp.float32, out_ref.dtype
    found = picks(pick_ref, share_ref)
    for pick, r, t, _ in found:
        rows_ref[r, :] = jnp.dot(pick, x_ref[t, :], preferred_element_type=f32).astype(bf)
    pre = contract(rows_ref[...], wg_ref[...], 1, 1)
    lift = contract(rows_ref[...], wu_ref[...], 1, 1)
    hidden = (pre / (1.0 + jnp.exp(-pre)) * lift).astype(bf)
    pre_ref[...] = pre
    lift_ref[...] = lift
    hid_ref[...] = hidden
    scale = jnp.concatenate([item[3] for item in found], axis=0)
    done = (jnp.dot(hidden, wd_ref[...], preferred_element_type=f32) * scale).astype(bf)
    lanes = wsd_ref.shape[0]
    both = jnp.dot(x_ref[...], ws_ref[...], preferred_element_type=f32)
    both_ref[...] = both
    pre, lift = both[:, :lanes], both[:, lanes:]
    hs_ref[...] = (pre / (1.0 + jnp.exp(-pre)) * lift).astype(bf)
    for pick, r, t, _ in found:
        shared = jnp.dot(hs_ref[t, :], wsd_ref[...], preferred_element_type=f32)
        out_ref[t, :] = (contract(pick, done[r, :], 0, 0) + shared).astype(bf)


def backward_kernel(
    c_ref, pick_ref, share_ref, pre_ref, lift_ref, both_ref, wg_ref, wu_ref, wd_ref, ws_ref, wsd_ref,
    dx_ref, drows_ref, dpre_ref, dlift_ref, dsh_ref,
):
    f32, bf = jnp.float32, dx_ref.dtype
    found = picks(pick_ref, share_ref)

    def gates(pre, lift, d_hidden):
        sigma = 1.0 / (1.0 + jnp.exp(-pre))
        d_pre = (d_hidden * lift * (sigma * (1.0 + pre * (1.0 - sigma)))).astype(bf)
        return d_pre, (d_hidden * (pre * sigma)).astype(bf)

    for pick, r, t, scale in found:
        taken = jnp.dot(pick, c_ref[t, :], preferred_element_type=f32)
        drows_ref[r, :] = (taken * scale).astype(bf)
    d_hidden = contract(drows_ref[...], wd_ref[...], 1, 1)
    d_pre, d_lift = gates(pre_ref[...], lift_ref[...], d_hidden)
    dpre_ref[...] = d_pre
    dlift_ref[...] = d_lift
    d_done = (contract(d_pre, wg_ref[...], 1, 0) + contract(d_lift, wu_ref[...], 1, 0)).astype(bf)
    lanes = wsd_ref.shape[0]
    d_shared = contract(c_ref[...], wsd_ref[...], 1, 1)
    d_pre, d_lift = gates(both_ref[:, :lanes], both_ref[:, lanes:], d_shared)
    dsh_ref[:, :lanes] = d_pre
    dsh_ref[:, lanes:] = d_lift
    for pick, r, t, _ in found:
        shared = contract(dsh_ref[t, :], ws_ref[...], 1, 1)
        dx_ref[t, :] = (contract(pick, d_done[r, :], 0, 0) + shared).astype(bf)


def by_tiles(kernel, name, micros, moving, fixed, outs, steps):
    def tile(shape):
        cut = (shape[0] // steps,) + tuple(shape[1:])
        return pl.BlockSpec(cut, lambda i: (i,) + (0,) * (len(shape) - 1))

    keep = lambda a: pl.BlockSpec(a.shape, lambda i: (0,) * a.ndim, pipeline_mode=pl.Buffered(1))
    return pl.pallas_call(
        kernel,
        grid=(steps,),
        out_shape=tuple(jax.ShapeDtypeStruct(s, d) for s, d in outs),
        in_specs=[tile(a.shape) for a in moving] + [keep(a) for a in fixed],
        out_specs=tuple(tile(s) for s, d in outs),
        compiler_params=pltpu.CompilerParams(vmem_limit_bytes=62 * 2**20),
        cost_estimate=busy(micros),
        name=name,
    )(*moving, *fixed)


def norm_back(values, gain, upstream):
    value, pull = jax.vjp(norm_apply, values, gain)
    return pull(upstream)


def block_body(
    tokens,
    norm_gain,
    query_proj,
    latent_proj,
    latent_gain,
    expand_proj,
    output_proj,
    mixer_gain,
    shared_gate,
    shared_up,
    shared_down,
    expert_gate,
    expert_up,
    expert_down,
    doc_starts,
    routes,
    gate_levels,
    cotangent,
):
    bf, f32 = jnp.bfloat16, jnp.float32
    seq = lax.axis_index("seq")
    fsdp = lax.axis_index("fsdp")
    both = ("seq", "fsdp")
    inputs = tokens[0].astype(f32)
    toks, width = inputs.shape
    n_dev = 32
    rows = query_proj.shape[0]
    latent_rows = expand_proj.shape[0]
    groups = rows // latent_rows
    n_q, n_o, n_l = query_proj.shape[1], output_proj.shape[1], latent_proj.shape[1]
    n_e = expand_proj.shape[1] // groups
    experts_count = 16
    capacity = 3 * toks * TOPK // (2 * experts_count)

    chosen = routes[0]
    levels = gate_levels[0]
    by_expert = jnp.sum(
        jnp.where(
            chosen.T[:, None, :] == jnp.arange(experts_count, dtype=jnp.int32)[None, :, None],
            levels.T[:, None, :],
            0,
        ),
        axis=0,
    )
    line = lambda v: jnp.pad(v, (0, toks - v.shape[0]))[None]
    info = jnp.concatenate(
        [
            by_expert.astype(bf),
            jnp.sum(levels, axis=1).astype(bf)[None],
            line(norm_gain),
            line(mixer_gain),
            line(latent_gain),
            jnp.zeros((rows - experts_count - 4, toks), bf),
        ],
        axis=0,
    )
    folded = jnp.concatenate(jnp.split(expand_proj, groups, axis=1), axis=0)
    aside = n_q + n_e + n_o + 5 * toks
    packed = jnp.concatenate(
        [
            query_proj,
            folded,
            output_proj,
            jnp.pad(latent_proj, ((0, 0), (0, 5 * toks - n_l))),
            info,
            jnp.zeros((rows, 2 * toks), bf),
        ],
        axis=1,
    )
    grouped = gather_all(packed, 1)
    grouped, held_cotangent = lax.optimization_barrier((grouped, cotangent[0]))
    all_info = grouped[:, :, :, aside : aside + toks].astype(f32).reshape(n_dev, rows, toks)
    gain_one = all_info[:, experts_count + 1, :rows].reshape(-1)
    gain_two = all_info[:, experts_count + 2, :rows].reshape(-1)
    gain_latent = all_info[:, experts_count + 3, :latent_rows].reshape(-1)
    blocks = grouped.reshape(n_dev, rows, -1)
    weights = blocks.reshape(width, -1)

    n_s = shared_down.shape[0]
    lanes = 128
    fill = lambda v: jnp.pad(v.reshape(rows, n_dev, n_s), ((0, 0), (0, 0), (0, lanes - n_s)))
    gate_up = jnp.concatenate([fill(shared_gate), fill(shared_up)], axis=2)
    w_shared = lax.all_to_all(
        jnp.swapaxes(gate_up, 0, 1), both, split_axis=0, concat_axis=0, tiled=True
    ).reshape(width, 2 * lanes)

    cot_all = lax.all_gather(held_cotangent, both, axis=0, tiled=True)

    normed = norm_apply(inputs, gain_one).astype(bf)
    query_raw = times_columns(normed, weights, 0, n_q // 512, 512).reshape(toks, H, DN + DR)
    latent_raw = times_columns(normed, weights, (n_q + n_e + n_o) // 512, 2, 512)[:, :n_l]
    latent = latent_raw[:, :KVL]
    latent_normed = norm_apply(latent, gain_latent).astype(bf)
    positions = seq * toks + jnp.arange(toks, dtype=jnp.int32)
    cosine, sine = rotary_tables(positions, DR)
    query = jnp.concatenate(
        [query_raw[:, :, :DN], rotate(query_raw[:, :, DN:], cosine[:, None, :], sine[:, None, :])],
        axis=2,
    ).astype(bf)
    key_rotary = rotate(latent_raw[:, KVL:], cosine, sine).astype(bf)
    own = jnp.concatenate([latent_normed, key_rotary, jnp.zeros((toks, 64), bf)], axis=1)
    pair = seq_swap(jnp.stack([own, own]), 4)
    pair = jnp.where(seq == 0, pair, pair[::-1]).reshape(2 * toks, -1)
    latent_full = pair[:, :KVL]
    rotary_full = pair[:, KVL : KVL + DR]
    expanded = times_folded(latent_full, blocks, latent_rows, n_q // n_e, n_e)
    expanded = expanded.reshape(2 * toks, H, DN + DV)
    keys, values = expanded[:, :, :DN], expanded[:, :, DN:]
    keys = jnp.concatenate(
        [keys, jnp.broadcast_to(rotary_full[:, None, :], (2 * toks, H, DR))], axis=2
    )
    documents = jnp.cumsum(doc_starts[0])
    key_spots = jnp.arange(2 * toks)
    own_documents = lax.dynamic_slice(documents, (seq * toks,), (toks,))
    allowed = (key_spots[None, :] <= positions[:, None]) & (
        documents[None, :] == own_documents[:, None]
    )
    score_scale = (DN + DR) ** (-0.5)
    scores = jnp.einsum("qhd,khd->hqk", query, keys, preferred_element_type=f32) * score_scale
    scores = jnp.where(allowed[None], scores, -1e30)
    raised = jnp.exp(scores - jnp.max(scores, axis=-1, keepdims=True))
    soft = raised / jnp.sum(raised, axis=-1, keepdims=True)
    soft_low = soft.astype(bf)
    mixed = jnp.einsum("hqk,khd->qhd", soft_low, values, preferred_element_type=f32).astype(bf)
    attended = mixed.reshape(toks, H * DV)
    middle = inputs + times_columns(attended, weights, (n_q + n_e) // 512, n_o // 512, 512)
    normed_two = norm_apply(middle, gain_two).astype(bf)

    gathered = gather_all(normed_two, 5)
    x_all = gathered.reshape(-1, width)
    level = lax.dynamic_index_in_dim(all_info, fsdp, axis=1, keepdims=False)
    mask = level > 0
    share = level / all_info[:, experts_count]
    slot = jnp.cumsum(mask.astype(jnp.int32), axis=1) - 1
    pair = lambda v: v.reshape(n_dev // 2, 2 * toks)
    slot = pair(slot + capacity * (jnp.arange(n_dev, dtype=jnp.int32)[:, None] % 2))
    pick = pair(mask)[:, None, :] & (
        slot[:, None, :] == jnp.arange(2 * capacity, dtype=jnp.int32)[None, :, None]
    )
    pick = pick.astype(bf)
    pair_share = pair(share)[:, None, :]
    weights_here = (
        expert_gate[0].T,
        expert_up[0].T,
        expert_down[0],
        w_shared,
        jnp.pad(shared_down, ((0, lanes - n_s), (0, 0))),
    )
    n_rows, n_h, steps = n_dev * capacity, expert_gate.shape[2], n_dev // 4
    out_parts, e_rows, e_pre, e_lift, e_hidden, s_both, s_hidden = by_tiles(
        forward_kernel,
        "experts_forward",
        40,
        (x_all, pick, pair_share),
        weights_here,
        (
            ((n_dev * toks, width), bf),
            ((n_rows, width), bf),
            ((n_rows, n_h), f32),
            ((n_rows, n_h), f32),
            ((n_rows, n_h), bf),
            ((n_dev * toks, 2 * lanes), f32),
            ((n_dev * toks, lanes), bf),
        ),
        steps,
    )
    layer_out = middle + lax.psum_scatter(
        out_parts, both, scatter_dimension=0, tiled=True
    ).astype(f32)
    grad_out = cotangent[0].astype(f32)
    d_parts, d_rows, d_pre, d_lift, d_shared = by_tiles(
        backward_kernel,
        "experts_backward",
        50,
        (cot_all, pick, pair_share, e_pre, e_lift, s_both),
        weights_here,
        (
            ((n_dev * toks, width), bf),
            ((n_rows, width), bf),
            ((n_rows, n_h), bf),
            ((n_rows, n_h), bf),
            ((n_dev * toks, 2 * lanes), bf),
        ),
        steps,
    )
    expert_down_grad = contract(e_hidden, d_rows, 0, 0)
    expert_gate_grad = contract(e_rows, d_pre, 0, 0)
    expert_up_grad = contract(e_rows, d_lift, 0, 0)
    shared_down_grad = contract(s_hidden, cot_all, 0, 0)[:n_s]
    shared_both_grad = contract(x_all, d_shared, 0, 0).astype(bf)
    expert_down_grad, expert_gate_grad, expert_up_grad, shared_down_grad, shared_both_grad, d_parts = (
        lax.optimization_barrier(
            (
                expert_down_grad,
                expert_gate_grad,
                expert_up_grad,
                shared_down_grad,
                shared_both_grad,
                d_parts,
            )
        )
    )
    d_normed_two = scatter_sum(d_parts.reshape(n_dev, toks, width), 7)
    shared_back = lax.all_to_all(
        shared_both_grad.reshape(n_dev, rows, 256), both, split_axis=0, concat_axis=0, tiled=True
    )
    shared_back = jnp.swapaxes(shared_back, 0, 1).astype(f32)
    shared_gate_grad = shared_back[:, :, :n_s].reshape(rows, n_dev * n_s)
    shared_up_grad = shared_back[:, :, lanes : lanes + n_s].reshape(rows, n_dev * n_s)

    d_middle_norm, mixer_gain_grad = norm_back(middle, gain_two, d_normed_two)
    d_middle = grad_out + d_middle_norm
    d_attn = d_middle.astype(bf)
    d_mixed = times_rows(d_attn, weights, (n_q + n_e) // n_o, n_o, 512).astype(bf).reshape(toks, H, DV)
    d_soft = jnp.einsum("qhd,khd->hqk", d_mixed, values, preferred_element_type=f32)
    delta = jnp.sum(soft * d_soft, axis=-1, keepdims=True)
    d_scores = (soft * (d_soft - delta)).astype(bf)
    d_values = jnp.einsum("hqk,qhd->khd", soft_low, d_mixed, preferred_element_type=f32).astype(bf)
    d_query = (
        jnp.einsum("hqk,khd->qhd", d_scores, keys, preferred_element_type=f32) * score_scale
    )
    d_keys = (
        jnp.einsum("hqk,qhd->khd", d_scores, query, preferred_element_type=f32) * score_scale
    )
    d_query_raw = (
        jnp.concatenate(
            [
                d_query[:, :, :DN],
                rotate(d_query[:, :, DN:], cosine[:, None, :], -sine[:, None, :]),
            ],
            axis=2,
        )
        .astype(bf)
        .reshape(toks, -1)
    )
    d_expanded = jnp.concatenate([d_keys[:, :, :DN].astype(bf), d_values], axis=2)
    d_expanded = d_expanded.reshape(2 * toks, -1)
    d_latent_pair = times_folded_back(d_expanded, blocks, latent_rows, n_q // n_e, n_e)
    d_rotary_pair = jnp.sum(d_keys[:, :, DN:], axis=1)
    d_pair = jnp.concatenate(
        [d_latent_pair, d_rotary_pair, jnp.zeros((2 * toks, 64), f32)], axis=1
    ).reshape(2, toks, -1)
    d_pair = jnp.sum(seq_swap(d_pair, 8), axis=0)
    d_latent_normed = d_pair[:, :KVL]
    d_key_rotary = rotate(d_pair[:, KVL : KVL + DR], cosine, -sine)
    d_latent, latent_gain_grad = norm_back(latent, gain_latent, d_latent_normed)
    d_latent_raw = jnp.concatenate([d_latent, d_key_rotary], axis=1).astype(bf)
    d_latent_wide = jnp.pad(d_latent_raw, ((0, 0), (0, 1024 - n_l)))
    d_normed = times_rows(d_query_raw, weights, 0, n_q, 512) + times_rows(
        d_latent_wide, weights, (n_q + n_e + n_o) // 1024, 1024, 512
    )
    d_inputs, norm_gain_grad = norm_back(inputs, gain_one, d_normed)
    input_grad = d_middle + d_inputs

    latent_gain_part = jnp.pad(
        latent_gain_grad.reshape(n_dev, latent_rows), ((0, 0), (0, rows - latent_rows))
    )
    gain_parts = jnp.stack(
        [
            norm_gain_grad.reshape(n_dev, rows),
            mixer_gain_grad.reshape(n_dev, rows),
            latent_gain_part,
        ],
        axis=2,
    )
    wide = 768
    gain_parts = jnp.pad(gain_parts, ((0, 0), (0, 0), (n_l, wide - n_l - 3))).astype(bf)
    grad_parts = packed_grads(
        n_dev,
        rows,
        latent_rows,
        normed.T,
        d_query_raw,
        latent_full.T,
        d_expanded,
        attended.T,
        d_attn,
        d_latent_wide[:, :wide],
        gain_parts,
    )
    grads = scatter_sum(grad_parts, 9)
    at_output = n_q + n_e
    at_latent = at_output + n_o
    at_gain = at_latent + n_l
    expand_out = jnp.concatenate(
        jnp.split(grads[:, n_q:at_output], groups, axis=0), axis=1
    )
    return (
        layer_out[None],
        input_grad[None],
        grads[:, at_gain],
        grads[:, :n_q],
        grads[:, at_latent:at_gain],
        grads[:latent_rows, at_gain + 2],
        expand_out,
        grads[:, at_output:at_latent],
        grads[:, at_gain + 1],
        shared_gate_grad,
        shared_up_grad,
        shared_down_grad,
        expert_gate_grad[None],
        expert_up_grad[None],
        expert_down_grad[None],
    )


def plain_body(
    tokens,
    norm_gain,
    query_proj,
    latent_proj,
    latent_gain,
    expand_proj,
    output_proj,
    mixer_gain,
    shared_gate,
    shared_up,
    shared_down,
    expert_gate,
    expert_up,
    expert_down,
    doc_starts,
    routes,
    gate_levels,
    cotangent,
):
    params = (
        norm_gain,
        query_proj,
        latent_proj,
        latent_gain,
        expand_proj,
        output_proj,
        mixer_gain,
        shared_gate,
        shared_up,
        shared_down,
        expert_gate,
        expert_up,
        expert_down,
    )
    saved = forward(params, tokens, doc_starts, routes, gate_levels)
    layer_out = saved["output"]
    input_grad, reduced, expert_gate_grad, expert_up_grad, expert_down_grad = backward(
        saved, cotangent
    )
    return (
        layer_out[None],
        input_grad[None],
        reduced[0],
        reduced[1],
        reduced[2],
        reduced[3],
        reduced[4],
        reduced[5],
        reduced[6],
        reduced[7],
        reduced[8],
        reduced[9],
        expert_gate_grad[None],
        expert_up_grad[None],
        expert_down_grad[None],
    )


def solution(mesh):
    in_specs = (
        P("fsdp", "seq", None),
        P(("seq", "fsdp")),
        P(("seq", "fsdp"), None),
        P(("seq", "fsdp"), None),
        P(("seq", "fsdp")),
        P(("seq", "fsdp"), None),
        P(("seq", "fsdp"), None),
        P(("seq", "fsdp")),
        P(("seq", "fsdp"), None),
        P(("seq", "fsdp"), None),
        P(("seq", "fsdp"), None),
        P("fsdp", None, "seq"),
        P("fsdp", None, "seq"),
        P("fsdp", "seq", None),
        P("fsdp", None),
        P("fsdp", "seq", None),
        P("fsdp", "seq", None),
        P("fsdp", "seq", None),
    )
    out_specs = (
        P("fsdp", "seq", None),
        P("fsdp", "seq", None),
        P(("seq", "fsdp")),
        P(("seq", "fsdp"), None),
        P(("seq", "fsdp"), None),
        P(("seq", "fsdp")),
        P(("seq", "fsdp"), None),
        P(("seq", "fsdp"), None),
        P(("seq", "fsdp")),
        P(("seq", "fsdp"), None),
        P(("seq", "fsdp"), None),
        P(("seq", "fsdp"), None),
        P("fsdp", None, "seq"),
        P("fsdp", None, "seq"),
        P("fsdp", "seq", None),
    )
    chosen = block_body if dict(mesh.shape) == {"seq": 2, "fsdp": 16} else plain_body
    return jax.shard_map(chosen, mesh=mesh, in_specs=in_specs, out_specs=out_specs, check_vma=False)
```

```python
import functools

import jax
import jax.numpy as jnp
from jax import lax
from jax.experimental import pallas as pl
from jax.experimental.pallas import tpu as pltpu
from jax.sharding import PartitionSpec as P


H = 16
DN = 128
DR = 64
DV = 128
KVL = 512
TOPK = 6


norm_epsilon = 1e-06
rotary_base = 10000.0


def norm_apply(values, gain):
    inverse = lax.rsqrt(jnp.mean(values * values, axis=-1, keepdims=True) + norm_epsilon)
    return values * inverse * gain


def sigmoid_linear(values):
    return values * jax.nn.sigmoid(values)


def rotary_tables(positions, width):
    halfway = width // 2
    frequency = rotary_base ** (-2.0 * jnp.arange(halfway, dtype=jnp.float32) / width)
    angles = positions.astype(jnp.float32)[:, None] * frequency[None, :]
    return (jnp.cos(angles), jnp.sin(angles))


def rotate(values, cosine, sine):
    halfway = values.shape[-1] // 2
    leading = values[..., :halfway]
    trailing = values[..., halfway:]
    return jnp.concatenate(
        [leading * cosine - trailing * sine, leading * sine + trailing * cosine], axis=-1
    )


def contract(left, right, left_dim, right_dim):
    return lax.dot_general(
        left, right, (((left_dim,), (right_dim,)), ((), ())), preferred_element_type=jnp.float32
    )


def silu_slope(values):
    sigma = jax.nn.sigmoid(values)
    return sigma * (1.0 + values * (1.0 - sigma))


def forward(params, tokens, doc_starts, routes, gate_levels):
    (
        norm_gain,
        query_proj,
        latent_proj,
        latent_gain,
        expand_proj,
        output_proj,
        mixer_gain,
        shared_gate,
        shared_up,
        shared_down,
        expert_gate,
        expert_up,
        expert_down,
    ) = params
    gathered = (
        lax.all_gather(norm_gain, ("seq", "fsdp"), axis=0, tiled=True),
        lax.all_gather(query_proj, ("seq", "fsdp"), axis=0, tiled=True),
        lax.all_gather(latent_proj, ("seq", "fsdp"), axis=0, tiled=True),
        lax.all_gather(latent_gain, ("seq", "fsdp"), axis=0, tiled=True),
        lax.all_gather(expand_proj, ("seq", "fsdp"), axis=0, tiled=True),
        lax.all_gather(output_proj, ("seq", "fsdp"), axis=0, tiled=True),
        lax.all_gather(mixer_gain, ("seq", "fsdp"), axis=0, tiled=True),
        lax.all_gather(shared_gate, ("seq", "fsdp"), axis=0, tiled=True),
        lax.all_gather(shared_up, ("seq", "fsdp"), axis=0, tiled=True),
        lax.all_gather(shared_down, ("seq", "fsdp"), axis=0, tiled=True),
    )
    inputs = tokens[0].astype(jnp.float32)
    tok_count = inputs.shape[0]
    normed = norm_apply(inputs, gathered[0].astype(jnp.float32)).astype(jnp.bfloat16)
    query_raw = jnp.dot(normed, gathered[1], preferred_element_type=jnp.float32).reshape(
        tok_count, H, DN + DR
    )
    latent_raw = jnp.dot(normed, gathered[2], preferred_element_type=jnp.float32)
    latent = latent_raw[:, :KVL]
    latent_normed = norm_apply(latent, gathered[3].astype(jnp.float32)).astype(jnp.bfloat16)
    expanded = jnp.dot(latent_normed, gathered[4], preferred_element_type=jnp.float32).reshape(
        tok_count, H, DN + DV
    )
    positions = lax.axis_index("seq") * tok_count + jnp.arange(tok_count, dtype=jnp.int32)
    cosine, sine = rotary_tables(positions, DR)
    query = jnp.concatenate(
        [query_raw[:, :, :DN], rotate(query_raw[:, :, DN:], cosine[:, None, :], sine[:, None, :])],
        axis=2,
    ).astype(jnp.bfloat16)
    key_rotary = rotate(latent_raw[:, KVL:], cosine, sine)
    keys = jnp.concatenate(
        [expanded[:, :, :DN], jnp.broadcast_to(key_rotary[:, None, :], (tok_count, H, DR))], axis=2
    ).astype(jnp.bfloat16)
    values = expanded[:, :, DN:].astype(jnp.bfloat16)
    head_query, head_keys, head_values = (
        lax.all_to_all(query, "seq", split_axis=1, concat_axis=0, tiled=True),
        lax.all_to_all(keys, "seq", split_axis=1, concat_axis=0, tiled=True),
        lax.all_to_all(values, "seq", split_axis=1, concat_axis=0, tiled=True),
    )
    documents = jnp.cumsum(doc_starts[0])
    spots = jnp.arange(documents.shape[0])
    allowed = (spots[None, :] <= spots[:, None]) & (documents[None, :] == documents[:, None])
    scores = jnp.einsum(
        "qhd,khd->hqk", head_query, head_keys, preferred_element_type=jnp.float32
    ) * (DN + DR) ** (-0.5)
    scores = jnp.where(allowed[None], scores, -1e30)
    raised = jnp.exp(scores - jnp.max(scores, axis=-1, keepdims=True))
    soft = raised / jnp.sum(raised, axis=-1, keepdims=True)
    soft_low = soft.astype(jnp.bfloat16)
    mixed = jnp.einsum(
        "hqk,khd->qhd", soft_low, head_values, preferred_element_type=jnp.float32
    ).astype(jnp.bfloat16)
    returned = lax.all_to_all(mixed, "seq", split_axis=0, concat_axis=1, tiled=True)
    attended = returned.reshape(tok_count, H * DV)
    middle = inputs + jnp.dot(attended, gathered[5], preferred_element_type=jnp.float32)
    normed_two = norm_apply(middle, gathered[6].astype(jnp.float32)).astype(jnp.bfloat16)
    shared_pre = jnp.dot(normed_two, gathered[7], preferred_element_type=jnp.float32)
    shared_lift = jnp.dot(normed_two, gathered[8], preferred_element_type=jnp.float32)
    shared_hidden = (sigmoid_linear(shared_pre) * shared_lift).astype(jnp.bfloat16)
    shared_result = jnp.dot(shared_hidden, gathered[9], preferred_element_type=jnp.float32)
    experts_count = lax.axis_size("fsdp")
    capacity = max(2, 3 * tok_count * TOPK // (2 * experts_count))
    chosen = routes[0].reshape(-1)
    matches = (chosen[:, None] == jnp.arange(experts_count, dtype=jnp.int32)[None, :]).astype(
        jnp.int32
    )
    earlier = jnp.sum((jnp.cumsum(matches, axis=0) - matches) * matches, axis=1)
    slots = chosen * capacity + earlier
    filled = (
        jnp.zeros((experts_count * capacity,), jnp.int32)
        .at[slots]
        .set(jnp.arange(chosen.shape[0], dtype=jnp.int32) + 1)
    )
    present = filled > 0
    sources = jnp.maximum(filled - 1, 0)
    outgoing = jnp.where(
        present[:, None], jnp.take(normed_two, sources // TOPK, axis=0), jnp.zeros((), jnp.bfloat16)
    )
    arrived = lax.all_to_all(
        outgoing.reshape(experts_count, capacity, -1),
        "fsdp",
        split_axis=0,
        concat_axis=0,
        tiled=True,
    )
    paired = lax.all_gather(arrived, "seq", axis=0, tiled=True)
    expert_rows = paired.reshape(-1, paired.shape[-1])
    gate_weight, up_weight, down_weight = (expert_gate[0], expert_up[0], expert_down[0])
    expert_pre = jnp.dot(expert_rows, gate_weight, preferred_element_type=jnp.float32)
    expert_lift = jnp.dot(expert_rows, up_weight, preferred_element_type=jnp.float32)
    expert_hidden = (sigmoid_linear(expert_pre) * expert_lift).astype(jnp.bfloat16)
    partial_out = jnp.dot(expert_hidden, down_weight, preferred_element_type=jnp.float32)
    summed = lax.psum_scatter(
        partial_out.reshape(paired.shape).astype(jnp.bfloat16),
        "seq",
        scatter_dimension=0,
        tiled=True,
    )
    results = lax.all_to_all(summed, "fsdp", split_axis=0, concat_axis=0, tiled=True)
    picked = jnp.take(results.reshape(experts_count * capacity, -1), slots, axis=0)
    picked = picked.astype(jnp.float32).reshape(tok_count, TOPK, -1)
    levels = gate_levels[0].astype(jnp.float32)
    gate_share = levels / jnp.sum(levels, axis=1, keepdims=True)
    routed = jnp.sum(gate_share[:, :, None] * picked, axis=1)
    output = middle + shared_result + routed
    return dict(
        gathered=gathered,
        inputs=inputs,
        normed=normed,
        latent=latent,
        latent_normed=latent_normed,
        cosine=cosine,
        sine=sine,
        head_query=head_query,
        head_keys=head_keys,
        head_values=head_values,
        soft=soft,
        soft_low=soft_low,
        attended=attended,
        middle=middle,
        normed_two=normed_two,
        shared_pre=shared_pre,
        shared_lift=shared_lift,
        shared_hidden=shared_hidden,
        capacity=capacity,
        slots=slots,
        present=present,
        sources=sources,
        expert_rows=expert_rows,
        expert_pre=expert_pre,
        expert_lift=expert_lift,
        expert_hidden=expert_hidden,
        expert_weights=(gate_weight, up_weight, down_weight),
        gate_share=gate_share,
        output=output,
    )


def backward(saved, cotangent):
    gate_weight, up_weight, down_weight = saved["expert_weights"]
    gathered = saved["gathered"]
    grad_out = cotangent[0].astype(jnp.float32)
    grad_low = cotangent[0]
    tok_count = grad_out.shape[0]
    experts_count = lax.axis_size("fsdp")
    capacity = saved["capacity"]
    d_picked = (saved["gate_share"][:, :, None] * grad_out[:, None, :]).astype(jnp.bfloat16)
    d_picked = d_picked.reshape(tok_count * TOPK, -1)
    d_slots = jnp.where(
        saved["present"][:, None],
        jnp.take(d_picked, saved["sources"], axis=0),
        jnp.zeros((), jnp.bfloat16),
    )
    d_arrived = lax.all_to_all(
        d_slots.reshape(experts_count, capacity, -1),
        "fsdp",
        split_axis=0,
        concat_axis=0,
        tiled=True,
    )
    d_paired = lax.all_gather(d_arrived, "seq", axis=0, tiled=True)
    d_expert_out = d_paired.reshape(-1, d_paired.shape[-1])
    expert_pre = saved["expert_pre"]
    expert_rows = saved["expert_rows"]
    expert_down_grad = contract(saved["expert_hidden"], d_expert_out, 0, 0)
    d_hidden = contract(d_expert_out, down_weight, 1, 1)
    d_pre = (d_hidden * saved["expert_lift"] * silu_slope(expert_pre)).astype(jnp.bfloat16)
    d_lift = (d_hidden * sigmoid_linear(expert_pre)).astype(jnp.bfloat16)
    expert_gate_grad = contract(expert_rows, d_pre, 0, 0)
    expert_up_grad = contract(expert_rows, d_lift, 0, 0)
    d_rows = contract(d_pre, gate_weight, 1, 1) + contract(d_lift, up_weight, 1, 1)
    d_summed = lax.psum_scatter(
        d_rows.reshape(d_paired.shape).astype(jnp.bfloat16), "seq", scatter_dimension=0, tiled=True
    )
    d_back = lax.all_to_all(d_summed, "fsdp", split_axis=0, concat_axis=0, tiled=True)
    d_routed = jnp.take(d_back.reshape(experts_count * capacity, -1), saved["slots"], axis=0)
    d_routed = jnp.sum(d_routed.astype(jnp.float32).reshape(tok_count, TOPK, -1), axis=1)
    shared_pre = saved["shared_pre"]
    normed_two = saved["normed_two"]
    shared_down_grad = contract(saved["shared_hidden"], grad_low, 0, 0)
    d_shared_hidden = contract(grad_low, gathered[9], 1, 1)
    d_shared_pre = (d_shared_hidden * saved["shared_lift"] * silu_slope(shared_pre)).astype(
        jnp.bfloat16
    )
    d_shared_lift = (d_shared_hidden * sigmoid_linear(shared_pre)).astype(jnp.bfloat16)
    shared_gate_grad = contract(normed_two, d_shared_pre, 0, 0)
    shared_up_grad = contract(normed_two, d_shared_lift, 0, 0)
    d_normed_two = (
        contract(d_shared_pre, gathered[7], 1, 1)
        + contract(d_shared_lift, gathered[8], 1, 1)
        + d_routed
    )
    mixer_value, mixer_pull = jax.vjp(norm_apply, saved["middle"], gathered[6].astype(jnp.float32))
    d_middle_norm, mixer_gain_grad = mixer_pull(d_normed_two)
    d_middle = grad_out + d_middle_norm
    d_attn = d_middle.astype(jnp.bfloat16)
    output_proj_grad = contract(saved["attended"], d_attn, 0, 0)
    d_attended = contract(d_attn, gathered[5], 1, 1).astype(jnp.bfloat16).reshape(tok_count, H, DV)
    d_mixed = lax.all_to_all(d_attended, "seq", split_axis=1, concat_axis=0, tiled=True)
    soft = saved["soft"]
    d_soft = jnp.einsum(
        "qhd,khd->hqk", d_mixed, saved["head_values"], preferred_element_type=jnp.float32
    )
    delta = jnp.sum(soft * d_soft, axis=-1, keepdims=True)
    d_scores = (soft * (d_soft - delta)).astype(jnp.bfloat16)
    score_scale = (DN + DR) ** (-0.5)
    d_head_values = jnp.einsum(
        "hqk,qhd->khd", saved["soft_low"], d_mixed, preferred_element_type=jnp.float32
    ).astype(jnp.bfloat16)
    d_head_query = (
        jnp.einsum("hqk,khd->qhd", d_scores, saved["head_keys"], preferred_element_type=jnp.float32)
        * score_scale
    ).astype(jnp.bfloat16)
    d_head_keys = (
        jnp.einsum(
            "hqk,qhd->khd", d_scores, saved["head_query"], preferred_element_type=jnp.float32
        )
        * score_scale
    ).astype(jnp.bfloat16)
    d_query, d_keys, d_values = (
        lax.all_to_all(d_head_query, "seq", split_axis=0, concat_axis=1, tiled=True),
        lax.all_to_all(d_head_keys, "seq", split_axis=0, concat_axis=1, tiled=True),
        lax.all_to_all(d_head_values, "seq", split_axis=0, concat_axis=1, tiled=True),
    )
    cosine = saved["cosine"]
    sine = saved["sine"]
    normed = saved["normed"]
    d_query_float = d_query.astype(jnp.float32)
    d_query_raw = (
        jnp.concatenate(
            [
                d_query_float[:, :, :DN],
                rotate(d_query_float[:, :, DN:], cosine[:, None, :], -sine[:, None, :]),
            ],
            axis=2,
        )
        .astype(jnp.bfloat16)
        .reshape(tok_count, -1)
    )
    query_proj_grad = contract(normed, d_query_raw, 0, 0)
    d_key_rotary = rotate(jnp.sum(d_keys[:, :, DN:].astype(jnp.float32), axis=1), cosine, -sine)
    d_expanded = jnp.concatenate([d_keys[:, :, :DN], d_values], axis=2).reshape(tok_count, -1)
    expand_proj_grad = contract(saved["latent_normed"], d_expanded, 0, 0)
    d_latent_normed = contract(d_expanded, gathered[4], 1, 1)
    latent_value, latent_pull = jax.vjp(
        norm_apply, saved["latent"], gathered[3].astype(jnp.float32)
    )
    d_latent, latent_gain_grad = latent_pull(d_latent_normed)
    d_latent_raw = jnp.concatenate([d_latent, d_key_rotary], axis=1).astype(jnp.bfloat16)
    latent_proj_grad = contract(normed, d_latent_raw, 0, 0)
    d_normed = contract(d_query_raw, gathered[1], 1, 1) + contract(d_latent_raw, gathered[2], 1, 1)
    input_value, input_pull = jax.vjp(norm_apply, saved["inputs"], gathered[0].astype(jnp.float32))
    d_inputs, norm_gain_grad = input_pull(d_normed)
    input_grad = d_middle + d_inputs
    reduced = (
        lax.psum_scatter(norm_gain_grad, ("seq", "fsdp"), scatter_dimension=0, tiled=True),
        lax.psum_scatter(query_proj_grad, ("seq", "fsdp"), scatter_dimension=0, tiled=True),
        lax.psum_scatter(latent_proj_grad, ("seq", "fsdp"), scatter_dimension=0, tiled=True),
        lax.psum_scatter(latent_gain_grad, ("seq", "fsdp"), scatter_dimension=0, tiled=True),
        lax.psum_scatter(expand_proj_grad, ("seq", "fsdp"), scatter_dimension=0, tiled=True),
        lax.psum_scatter(output_proj_grad, ("seq", "fsdp"), scatter_dimension=0, tiled=True),
        lax.psum_scatter(mixer_gain_grad, ("seq", "fsdp"), scatter_dimension=0, tiled=True),
        lax.psum_scatter(shared_gate_grad, ("seq", "fsdp"), scatter_dimension=0, tiled=True),
        lax.psum_scatter(shared_up_grad, ("seq", "fsdp"), scatter_dimension=0, tiled=True),
        lax.psum_scatter(shared_down_grad, ("seq", "fsdp"), scatter_dimension=0, tiled=True),
    )
    return (input_grad, reduced, expert_gate_grad, expert_up_grad, expert_down_grad)


MESH = pl.DeviceIdType.MESH

def busy(micros):
    return pl.CostEstimate(flops=0, bytes_accessed=int(micros * 3.5e6), transcendentals=0)


def coords():
    seq = lax.axis_index("seq")
    fsdp = lax.axis_index("fsdp")
    return seq, lax.rem(fsdp // 2, 2), fsdp // 4, lax.rem(fsdp, 2)

def device(x, y, z, c):
    return (x, (z * 2 + y) * 2 + c)

def place(x, y, z, c):
    return x * 16 + z * 4 + y * 2 + c

def greet(x, y, z, c):
    bar = pltpu.get_barrier_semaphore()
    for dev in (device(1 - x, y, z, c), device(x, 1 - y, z, c), device(x, y, z, 1 - c)):
        pl.semaphore_signal(bar, inc=1, device_id=dev, device_id_type=MESH)
    @pl.when(z > 0)
    def _():
        pl.semaphore_signal(bar, inc=1, device_id=device(x, y, z - 1, c), device_id_type=MESH)
    @pl.when(z < 3)
    def _():
        pl.semaphore_signal(bar, inc=1, device_id=device(x, y, z + 1, c), device_id_type=MESH)
    pl.semaphore_wait(bar, jnp.where((z > 0) & (z < 3), 5, 4))

def remote(src, dst, ss, rs, dev):
    return pltpu.make_async_remote_copy(src_ref=src, dst_ref=dst, send_sem=ss, recv_sem=rs, device_id=dev, device_id_type=MESH)

def near_order(z):
    w = jnp.where
    first = w(z == 0, 1, w(z == 1, 0, w(z == 2, 1, 2)))
    second = w(z == 0, 2, w(z == 1, 2, w(z == 2, 3, 1)))
    third = w(z == 0, 3, w(z == 1, 3, 0))
    return (first, second, third)

def ag_kernel(half, x_ref, o_ref, zs, zr, xs, xr, ys, yr, das, dar, dbs, dbr, cs, cr, ls):
    x, y, z, c = coords()
    greet(x, y, z, c)
    xm, ym, cm = device(1 - x, y, z, c), device(x, 1 - y, z, c), device(x, y, z, 1 - c)
    lo, hi = pl.ds(0, half), pl.ds(half, half)
    me = o_ref.at[place(x, y, z, c)]
    order = (z,) + near_order(z)
    sends = []
    local = pltpu.make_async_copy(x_ref, me, ls)
    local.start()
    def up(src, zz, sem):
        return remote(src, o_ref.at[place(x, y, zz, c)], zs.at[sem], zr.at[zz], device(x, y, z + 1, c))
    def down(src, zz, sem):
        return remote(src, o_ref.at[place(x, y, zz, c)], zs.at[sem], zr.at[zz], device(x, y, z - 1, c))
    @pl.when(z < 3)
    def _():
        up(x_ref, z, 0).start()
    @pl.when(z > 0)
    def _():
        down(x_ref, z, 1).start()
    def blk(dx, dy, zz, cc=None):
        return o_ref.at[place(jnp.abs(x - dx), jnp.abs(y - dy), zz, c if cc is None else cc)]
    def xsend(j):
        b = x_ref if j == 0 else blk(0, 0, order[j])
        return remote(b, blk(0, 0, order[j]), xs.at[j], xr.at[j], xm)
    def ysend(j):
        b = x_ref if j == 0 else blk(0, 0, order[j])
        return remote(b, blk(0, 0, order[j]), ys.at[j], yr.at[j], ym)
    def xrecv(j):
        b = blk(1, 0, order[j])
        return remote(b, b, xs.at[j], xr.at[j], xm)
    def yrecv(j):
        b = blk(0, 1, order[j])
        return remote(b, b, ys.at[j], yr.at[j], ym)
    def dasend(j):
        b = blk(1, 0, order[j]).at[lo]
        return remote(b, b, das.at[j], dar.at[j], ym)
    def dbsend(j):
        b = blk(0, 1, order[j]).at[hi]
        return remote(b, b, dbs.at[j], dbr.at[j], xm)
    def darecv(j):
        b = blk(1, 1, order[j]).at[lo]
        return remote(b, b, das.at[j], dar.at[j], ym)
    def dbrecv(j):
        b = blk(1, 1, order[j]).at[hi]
        return remote(b, b, dbs.at[j], dbr.at[j], xm)
    def csend(j, q):
        dx, dy = q % 2, q // 2
        b = blk(dx, dy, order[j])
        src = x_ref if (j == 0 and q == 0) else b
        return remote(src, b, cs.at[j * 4 + q], cr.at[j * 4 + q], cm)
    def crecv(j, q):
        b = blk(q % 2, q // 2, order[j], 1 - c)
        return remote(b, b, cs.at[j * 4 + q], cr.at[j * 4 + q], cm)
    def second(j):
        xrecv(j).wait_recv()
        dasend(j).start()
        csend(j, 1).start()
        yrecv(j).wait_recv()
        dbsend(j).start()
        csend(j, 2).start()
    def third(j):
        darecv(j).wait_recv()
        dbrecv(j).wait_recv()
        csend(j, 3).start()
    xsend(0).start()
    ysend(0).start()
    csend(0, 0).start()
    for j in (1, 2, 3):
        zz = order[j]
        b = o_ref.at[place(x, y, zz, c)]
        remote(b, b, zs.at[0], zr.at[zz], cm).wait_recv()
        @pl.when((zz < z) & (z < 3))
        def _():
            up(b, zz, j + 1).start()
        @pl.when((zz > z) & (z > 0))
        def _():
            down(b, zz, j + 1).start()
        xsend(j).start()
        ysend(j).start()
        csend(j, 0).start()
        second(j - 1)
        if j > 1:
            third(j - 2)
    second(3)
    third(2)
    third(3)
    local.wait()
    @pl.when(z < 3)
    def _():
        up(x_ref, z, 0).wait_send()
    @pl.when(z > 0)
    def _():
        down(x_ref, z, 1).wait_send()
    for j in range(4):
        if j:
            zz = order[j]
            b = o_ref.at[place(x, y, zz, c)]
            @pl.when((zz < z) & (z < 3))
            def _():
                up(b, zz, j + 1).wait_send()
            @pl.when((zz > z) & (z > 0))
            def _():
                down(b, zz, j + 1).wait_send()
        xsend(j).wait_send()
        ysend(j).wait_send()
        dasend(j).wait_send()
        dbsend(j).wait_send()
        for q in range(4):
            csend(j, q).wait_send()
            crecv(j, q).wait_recv()

DMA = pltpu.SemaphoreType.DMA

def gather_all(block, cid):
    rows, cols = block.shape
    grouped = (rows // 8, 8, cols)
    out = pl.pallas_call(
        functools.partial(ag_kernel, rows // 16),
        out_shape=jax.ShapeDtypeStruct((32,) + grouped, block.dtype),
        in_specs=[pl.BlockSpec(memory_space=pl.ANY)],
        out_specs=pl.BlockSpec(memory_space=pl.ANY),
        scratch_shapes=[DMA((5,)), DMA((4,))] + [DMA((4,))] * 8 + [DMA((16,)), DMA((16,)), DMA],
        compiler_params=pltpu.CompilerParams(
            collective_id=cid, has_side_effects=True, vmem_limit_bytes=60 * 2**20
        ),
        cost_estimate=busy(20 + block.size * block.dtype.itemsize / 8e3 ),
        name="gather_rows",
    )(block.reshape(grouped))
    return out


def far_order(z):
    w = jnp.where
    first = w(z < 2, 3, 0)
    second = w(z == 0, 2, w(z == 1, 0, w(z == 2, 3, 1)))
    third = w(z == 0, 1, w(z == 1, 2, w(z == 2, 1, 2)))
    return (first, second, third, z)

def rs_kernel(half, p_ref, o_ref, acc, cl, lxa, lya2, lyb, lxb2, zl, ls, cs, cr, xas, xar, ya2s, ya2r, ybs, ybr, xb2s, xb2r, zs, zr):
    x, y, z, c = coords()
    greet(x, y, z, c)
    xm, ym, cm = device(1 - x, y, z, c), device(x, 1 - y, z, c), device(x, y, z, 1 - c)
    order = far_order(z)
    rows = 2 * half
    lo, hi = pl.ds(0, half), pl.ds(half, half)
    def add(dst, at, src, src_at, count):
        def body(i, carry):
            d = dst.at[pl.ds(at + 2 * i, 2)]
            s = src.at[pl.ds(src_at + 2 * i, 2)]
            d[...] = (d[...].astype(jnp.float32) + s[...].astype(jnp.float32)).astype(d.dtype)
            return carry
        lax.fori_loop(0, count // 2, body, 0)
    def blk(q, zz, cc):
        return p_ref.at[place(jnp.abs(x - q % 2), jnp.abs(y - q // 2), zz, cc)]
    def load(j, q):
        return pltpu.make_async_copy(blk(q, order[j], c), acc.at[j, q], ls.at[j * 4 + q])
    def csend(j, q):
        return remote(blk(q, order[j], 1 - c), cl.at[j, q], cs.at[j * 4 + q], cr.at[j * 4 + q], cm)
    def xa(j, i):
        return remote(acc.at[j, 1 + 2 * i, lo], lxa.at[j, i], xas.at[j, i], xar.at[j, i], xm)
    def yb(j, i):
        return remote(acc.at[j, 2 + i, hi], lyb.at[j, i], ybs.at[j, i], ybr.at[j, i], ym)
    def ya2(j):
        return remote(acc.at[j, 2, lo], lya2.at[j], ya2s.at[j], ya2r.at[j], ym)
    def xb2(j):
        return remote(acc.at[j, 1, hi], lxb2.at[j], xb2s.at[j], xb2r.at[j], xm)
    firsts = (1, 3, 2, 0)
    for j in range(4):
        for q in firsts:
            csend(j, q).start()
            load(j, q).start()
    def one(j):
        for q in firsts:
            load(j, q).wait()
            csend(j, q).wait_recv()
            add(acc.at[j, q], 0, cl.at[j, q], 0, rows)
            if q == 1:
                xa(j, 0).start()
            if q == 3:
                xa(j, 1).start()
                yb(j, 1).start()
            if q == 2:
                yb(j, 0).start()
    def two(j):
        xa(j, 1).wait_recv()
        add(acc.at[j, 2], 0, lxa.at[j, 1], 0, half)
        ya2(j).start()
        yb(j, 1).wait_recv()
        add(acc.at[j, 1], half, lyb.at[j, 1], 0, half)
        xb2(j).start()
        xa(j, 0).wait_recv()
        add(acc.at[j, 0], 0, lxa.at[j, 0], 0, half)
        yb(j, 0).wait_recv()
        add(acc.at[j, 0], half, lyb.at[j, 0], 0, half)
    def zin(slot):
        return remote(zl.at[slot], zl.at[slot], zs.at[0], zr.at[slot], cm)
    def zout_up(j):
        return remote(acc.at[j, 0], zl.at[order[j]], zs.at[j], zr.at[order[j]], device(x, y, z + 1, c))
    def zout_down(j):
        slot = jnp.where(order[j] == z - 1, 4, order[j])
        return remote(acc.at[j, 0], zl.at[slot], zs.at[j], zr.at[slot], device(x, y, z - 1, c))
    def three(j):
        ya2(j).wait_recv()
        add(acc.at[j, 0], 0, lya2.at[j], 0, half)
        xb2(j).wait_recv()
        add(acc.at[j, 0], half, lxb2.at[j], 0, half)
        zz = order[j]
        if j < 3:
            @pl.when(((zz > z) & (z > 0)) | ((zz < z) & (z < 3)))
            def _():
                zin(zz).wait_recv()
                add(acc.at[j, 0], 0, zl.at[zz], 0, rows)
            @pl.when(zz > z)
            def _():
                zout_up(j).start()
            @pl.when(zz < z)
            def _():
                zout_down(j).start()
        else:
            @pl.when(z > 0)
            def _():
                zin(z).wait_recv()
                add(acc.at[j, 0], 0, zl.at[z], 0, rows)
            @pl.when(z < 3)
            def _():
                zin(4).wait_recv()
                add(acc.at[j, 0], 0, zl.at[4], 0, rows)
            def body(i, carry):
                o_ref[pl.ds(2 * i, 2)] = acc[3, 0, pl.ds(2 * i, 2)].astype(o_ref.dtype)
                return carry
            lax.fori_loop(0, rows // 2, body, 0)
    one(0)
    two(0)
    one(1)
    three(0)
    two(1)
    one(2)
    three(1)
    two(2)
    one(3)
    three(2)
    two(3)
    three(3)
    for j in range(4):
        for q in range(4):
            csend(j, q).wait_send()
        for i in range(2):
            xa(j, i).wait_send()
            yb(j, i).wait_send()
        ya2(j).wait_send()
        xb2(j).wait_send()
        if j < 3:
            zz = order[j]
            @pl.when(zz > z)
            def _():
                zout_up(j).wait_send()
            @pl.when(zz < z)
            def _():
                zout_down(j).wait_send()

def scatter_sum(parts, cid):
    _, rows, cols = parts.shape
    bf = parts.dtype
    whole, half = (rows // 8, 8, cols), (rows // 16, 8, cols)
    out = pl.pallas_call(
        functools.partial(rs_kernel, rows // 16),
        out_shape=jax.ShapeDtypeStruct(whole, jnp.float32),
        in_specs=[pl.BlockSpec(memory_space=pl.ANY)],
        out_specs=pl.BlockSpec(memory_space=pltpu.VMEM),
        scratch_shapes=[
            pltpu.VMEM((4, 4) + whole, bf),
            pltpu.VMEM((4, 4) + whole, bf),
            pltpu.VMEM((4, 2) + half, bf),
            pltpu.VMEM((4,) + half, bf),
            pltpu.VMEM((4, 2) + half, bf),
            pltpu.VMEM((4,) + half, bf),
            pltpu.VMEM((5,) + whole, bf),
            DMA((16,)), DMA((16,)), DMA((16,)), DMA((4, 2)), DMA((4, 2)), DMA((4,)), DMA((4,)),
            DMA((4, 2)), DMA((4, 2)), DMA((4,)), DMA((4,)), DMA((3,)), DMA((5,)),
        ],
        compiler_params=pltpu.CompilerParams(
            collective_id=cid, has_side_effects=True, vmem_limit_bytes=60 * 2**20
        ),
        cost_estimate=busy(20 + rows * cols * bf.itemsize / 8e3),
        name="scatter_sum",
    )(parts.reshape((32,) + whole))
    return out.reshape(rows, cols)


def spread_kernel(x_ref, o_ref, ls, ss, rs):
    x, y, z, c = coords()
    me = place(x, y, z, c)
    n_dev = x_ref.shape[0]

    def far(k):
        kx, kz, ky, kc = k // 16, lax.rem(k // 4, 4), lax.rem(k // 2, 2), lax.rem(k, 2)
        return jnp.abs(x - kx), jnp.abs(y - ky), lax.rem(z + kz, 4), jnp.abs(c - kc)

    bar = pltpu.get_barrier_semaphore()

    def greet_one(k, carry):
        pl.semaphore_signal(bar, inc=1, device_id=device(*far(k)), device_id_type=MESH)
        return carry

    lax.fori_loop(1, n_dev, greet_one, 0)

    pl.semaphore_wait(bar, n_dev - 1)

    def send(k):
        to = far(k)
        return remote(x_ref.at[place(*to)], o_ref.at[me], ss.at[k], rs.at[k], device(*to))

    def start(k, carry):
        send(k).start()
        return carry

    lax.fori_loop(1, n_dev, start, 0)
    local = pltpu.make_async_copy(x_ref.at[me], o_ref.at[me], ls)
    local.start()
    local.wait()

    def finish(k, carry):
        send(k).wait()
        return carry

    lax.fori_loop(1, n_dev, finish, 0)


def spread_all(blocks, cid):
    count, rows, cols = blocks.shape
    grouped = (count, rows // 8, 8, cols)
    out = pl.pallas_call(
        spread_kernel,
        out_shape=jax.ShapeDtypeStruct(grouped, blocks.dtype),
        in_specs=[pl.BlockSpec(memory_space=pl.ANY)],
        out_specs=pl.BlockSpec(memory_space=pl.ANY),
        scratch_shapes=[DMA, DMA((32,)), DMA((32,))],
        compiler_params=pltpu.CompilerParams(
            collective_id=cid, has_side_effects=True, vmem_limit_bytes=60 * 2**20
        ),
        cost_estimate=busy(25),
        name="spread_all",
    )(blocks.reshape(grouped))
    return out.reshape(blocks.shape)


def swap_kernel(x_ref, o_ref, ls, ss, rs):
    x, y, z, c = coords()
    mate = device(1 - x, y, z, c)
    bar = pltpu.get_barrier_semaphore()
    pl.semaphore_signal(bar, inc=1, device_id=mate, device_id_type=MESH)
    pl.semaphore_wait(bar, 1)
    out = remote(x_ref.at[1 - x], o_ref.at[1], ss, rs, mate)
    out.start()
    local = pltpu.make_async_copy(x_ref.at[x], o_ref.at[0], ls)
    local.start()
    local.wait()
    out.wait()


def seq_swap(pieces, cid):
    count, rows, cols = pieces.shape
    grouped = (count, rows // 8, 8, cols)
    out = pl.pallas_call(
        swap_kernel,
        out_shape=jax.ShapeDtypeStruct(grouped, pieces.dtype),
        in_specs=[pl.BlockSpec(memory_space=pl.ANY)],
        out_specs=pl.BlockSpec(memory_space=pl.ANY),
        scratch_shapes=[DMA, DMA, DMA],
        compiler_params=pltpu.CompilerParams(
            collective_id=cid, has_side_effects=True, vmem_limit_bytes=60 * 2**20
        ),
        cost_estimate=busy(8),
        name="seq_swap",
    )(pieces.reshape(grouped))
    return out.reshape(pieces.shape)


def columns_kernel(x_ref, w_ref, o_ref):
    o_ref[...] = jnp.dot(x_ref[...], w_ref[...], preferred_element_type=jnp.float32)


def times_columns(rows_in, weights, first, count, tile):
    m, k = rows_in.shape
    return pl.pallas_call(
        columns_kernel,
        grid=(count,),
        out_shape=jax.ShapeDtypeStruct((m, count * tile), jnp.float32),
        in_specs=[
            pl.BlockSpec((m, k), lambda i: (0, 0)),
            pl.BlockSpec((k, tile), lambda i: (0, first + i)),
        ],
        out_specs=pl.BlockSpec((m, tile), lambda i: (0, i)),
        compiler_params=pltpu.CompilerParams(vmem_limit_bytes=48 * 2**20),
        name="times_columns",
    )(rows_in, weights)


def rows_kernel(x_ref, w_ref, o_ref):
    o_ref[...] = contract(x_ref[...], w_ref[...], 1, 1)


def times_rows(rows_in, weights, at, width, tile):
    m = rows_in.shape[0]
    k = weights.shape[0]
    return pl.pallas_call(
        rows_kernel,
        grid=(k // tile,),
        out_shape=jax.ShapeDtypeStruct((m, k), jnp.float32),
        in_specs=[
            pl.BlockSpec((m, width), lambda i: (0, 0)),
            pl.BlockSpec((tile, width), lambda i: (i, at)),
        ],
        out_specs=pl.BlockSpec((m, tile), lambda i: (0, i)),
        compiler_params=pltpu.CompilerParams(vmem_limit_bytes=48 * 2**20),
        name="times_rows",
    )(rows_in, weights)


def expand_kernel(x_ref, w_ref, o_ref):
    weight = w_ref[...].reshape(x_ref.shape[1], w_ref.shape[2])
    o_ref[...] = jnp.dot(x_ref[...], weight, preferred_element_type=jnp.float32).astype(o_ref.dtype)


def times_folded(rows_in, weights, fold, at, width):
    m, k = rows_in.shape
    groups = weights.shape[1] // fold
    return pl.pallas_call(
        expand_kernel,
        grid=(groups,),
        out_shape=jax.ShapeDtypeStruct((m, groups * width), jnp.bfloat16),
        in_specs=[
            pl.BlockSpec((m, k), lambda g: (0, 0)),
            pl.BlockSpec((weights.shape[0], fold, width), lambda g: (0, g, at)),
        ],
        out_specs=pl.BlockSpec((m, width), lambda g: (0, g)),
        compiler_params=pltpu.CompilerParams(vmem_limit_bytes=48 * 2**20),
        name="times_folded",
    )(rows_in, weights)


def expand_back_kernel(x_ref, w_ref, o_ref):
    weight = w_ref[...].reshape(o_ref.shape[1], w_ref.shape[2])

    @pl.when(pl.program_id(0) == 0)
    def _():
        o_ref[...] = jnp.zeros_like(o_ref)

    o_ref[...] += contract(x_ref[...], weight, 1, 1)


def times_folded_back(rows_in, weights, fold, at, width):
    m = rows_in.shape[0]
    k = weights.shape[0] * fold
    groups = weights.shape[1] // fold
    return pl.pallas_call(
        expand_back_kernel,
        grid=(groups,),
        out_shape=jax.ShapeDtypeStruct((m, k), jnp.float32),
        in_specs=[
            pl.BlockSpec((m, width), lambda g: (0, g)),
            pl.BlockSpec((weights.shape[0], fold, width), lambda g: (0, g, at)),
        ],
        out_specs=pl.BlockSpec((m, k), lambda g: (0, 0)),
        compiler_params=pltpu.CompilerParams(vmem_limit_bytes=48 * 2**20),
        name="times_folded_back",
    )(rows_in, weights)


def grads_kernel(
    tile, n_q, n_e, n_o, fold, normed_ref, dq_ref, full_ref, dexp_ref, att_ref, dattn_ref, dlat_ref, gain_ref, o_ref
):
    t = pl.program_id(0)
    n_dev, rows, _ = o_ref.shape
    t_q, t_e, t_o = n_q // tile, n_e // tile, n_o // tile

    def cut(ref, i):
        return ref[:, pl.ds(pl.multiple_of(i * tile, tile), tile)]

    def put(left, right):
        done = jnp.dot(left, right, preferred_element_type=jnp.float32).astype(o_ref.dtype)
        return done.reshape(n_dev, done.shape[0] // n_dev, tile)

    @pl.when(t < t_q)
    def _():
        o_ref[...] = put(normed_ref[...], cut(dq_ref, t))

    @pl.when((t >= t_q) & (t < t_q + t_e))
    def _():
        for g in range(rows // fold):
            part = cut(dexp_ref, g * t_e + t - t_q)
            o_ref[:, g * fold : (g + 1) * fold, :] = put(full_ref[...], part)

    @pl.when((t >= t_q + t_e) & (t < t_q + t_e + t_o))
    def _():
        o_ref[...] = put(att_ref[...], cut(dattn_ref, t - t_q - t_e))

    @pl.when(t >= t_q + t_e + t_o)
    def _():
        i = t - t_q - t_e - t_o
        o_ref[...] = put(normed_ref[...], cut(dlat_ref, i)) + cut_gain(gain_ref, i, tile)


def cut_gain(ref, i, tile):
    return ref[:, :, pl.ds(pl.multiple_of(i * tile, tile), tile)]


def packed_grads(n_dev, rows, fold, normed, dq, full, dexp, att, dattn, dlat, gain):
    tile = 256
    n_q, n_e, n_o, n_l = dq.shape[1], dexp.shape[1] // (rows // fold), dattn.shape[1], dlat.shape[1]
    cols = n_q + n_e + n_o + n_l
    whole = lambda a: pl.BlockSpec(a.shape, lambda i: (0,) * a.ndim)
    operands = (normed, dq, full, dexp, att, dattn, dlat, gain)
    return pl.pallas_call(
        functools.partial(grads_kernel, tile, n_q, n_e, n_o, fold),
        grid=(cols // tile,),
        out_shape=jax.ShapeDtypeStruct((n_dev, rows, cols), jnp.bfloat16),
        in_specs=[whole(a) for a in operands],
        out_specs=pl.BlockSpec((n_dev, rows, tile), lambda i: (0, 0, i)),
        compiler_params=pltpu.CompilerParams(vmem_limit_bytes=56 * 2**20),
        name="packed_grads",
    )(*operands)


def picks(pick_ref, share_ref):
    pairs, slots, toks = pick_ref.shape
    found = []
    for p in range(pairs):
        pick = pick_ref[p]
        scale = jnp.sum(pick.astype(jnp.float32) * share_ref[p], axis=1, keepdims=True)
        r, t = slice(p * slots, (p + 1) * slots), slice(p * toks, (p + 1) * toks)
        found.append((pick, r, t, scale))
    return found


def forward_kernel(
    x_ref, pick_ref, share_ref, wg_ref, wu_ref, wd_ref, ws_ref, wsd_ref,
    out_ref, rows_ref, pre_ref, lift_ref, hid_ref, both_ref, hs_ref,
):
    f32, bf = jnp.float32, out_ref.dtype
    found = picks(pick_ref, share_ref)
    for pick, r, t, _ in found:
        rows_ref[r, :] = jnp.dot(pick, x_ref[t, :], preferred_element_type=f32).astype(bf)
    pre = contract(rows_ref[...], wg_ref[...], 1, 1)
    lift = contract(rows_ref[...], wu_ref[...], 1, 1)
    hidden = (pre / (1.0 + jnp.exp(-pre)) * lift).astype(bf)
    pre_ref[...] = pre
    lift_ref[...] = lift
    hid_ref[...] = hidden
    scale = jnp.concatenate([item[3] for item in found], axis=0)
    done = (jnp.dot(hidden, wd_ref[...], preferred_element_type=f32) * scale).astype(bf)
    lanes = wsd_ref.shape[0]
    both = jnp.dot(x_ref[...], ws_ref[...], preferred_element_type=f32)
    both_ref[...] = both
    pre, lift = both[:, :lanes], both[:, lanes:]
    hs_ref[...] = (pre / (1.0 + jnp.exp(-pre)) * lift).astype(bf)
    for pick, r, t, _ in found:
        shared = jnp.dot(hs_ref[t, :], wsd_ref[...], preferred_element_type=f32)
        out_ref[t, :] = (contract(pick, done[r, :], 0, 0) + shared).astype(bf)


def backward_kernel(
    c_ref, pick_ref, share_ref, pre_ref, lift_ref, both_ref, wg_ref, wu_ref, wd_ref, ws_ref, wsd_ref,
    dx_ref, drows_ref, dpre_ref, dlift_ref, dsh_ref,
):
    f32, bf = jnp.float32, dx_ref.dtype
    found = picks(pick_ref, share_ref)

    def gates(pre, lift, d_hidden):
        sigma = 1.0 / (1.0 + jnp.exp(-pre))
        d_pre = (d_hidden * lift * (sigma * (1.0 + pre * (1.0 - sigma)))).astype(bf)
        return d_pre, (d_hidden * (pre * sigma)).astype(bf)

    for pick, r, t, scale in found:
        taken = jnp.dot(pick, c_ref[t, :], preferred_element_type=f32)
        drows_ref[r, :] = (taken * scale).astype(bf)
    d_hidden = contract(drows_ref[...], wd_ref[...], 1, 1)
    d_pre, d_lift = gates(pre_ref[...], lift_ref[...], d_hidden)
    dpre_ref[...] = d_pre
    dlift_ref[...] = d_lift
    d_done = (contract(d_pre, wg_ref[...], 1, 0) + contract(d_lift, wu_ref[...], 1, 0)).astype(bf)
    lanes = wsd_ref.shape[0]
    d_shared = contract(c_ref[...], wsd_ref[...], 1, 1)
    d_pre, d_lift = gates(both_ref[:, :lanes], both_ref[:, lanes:], d_shared)
    dsh_ref[:, :lanes] = d_pre
    dsh_ref[:, lanes:] = d_lift
    for pick, r, t, _ in found:
        shared = contract(dsh_ref[t, :], ws_ref[...], 1, 1)
        dx_ref[t, :] = (contract(pick, d_done[r, :], 0, 0) + shared).astype(bf)


def by_tiles(kernel, name, micros, moving, fixed, outs, steps):
    def tile(shape):
        cut = (shape[0] // steps,) + tuple(shape[1:])
        return pl.BlockSpec(cut, lambda i: (i,) + (0,) * (len(shape) - 1))

    keep = lambda a: pl.BlockSpec(a.shape, lambda i: (0,) * a.ndim, pipeline_mode=pl.Buffered(1))
    return pl.pallas_call(
        kernel,
        grid=(steps,),
        out_shape=tuple(jax.ShapeDtypeStruct(s, d) for s, d in outs),
        in_specs=[tile(a.shape) for a in moving] + [keep(a) for a in fixed],
        out_specs=tuple(tile(s) for s, d in outs),
        compiler_params=pltpu.CompilerParams(vmem_limit_bytes=62 * 2**20),
        cost_estimate=busy(micros),
        name=name,
    )(*moving, *fixed)


def norm_back(values, gain, upstream):
    value, pull = jax.vjp(norm_apply, values, gain)
    return pull(upstream)


def block_body(
    tokens,
    norm_gain,
    query_proj,
    latent_proj,
    latent_gain,
    expand_proj,
    output_proj,
    mixer_gain,
    shared_gate,
    shared_up,
    shared_down,
    expert_gate,
    expert_up,
    expert_down,
    doc_starts,
    routes,
    gate_levels,
    cotangent,
):
    bf, f32 = jnp.bfloat16, jnp.float32
    seq = lax.axis_index("seq")
    fsdp = lax.axis_index("fsdp")
    both = ("seq", "fsdp")
    inputs = tokens[0].astype(f32)
    toks, width = inputs.shape
    n_dev = 32
    rows = query_proj.shape[0]
    latent_rows = expand_proj.shape[0]
    groups = rows // latent_rows
    n_q, n_o, n_l = query_proj.shape[1], output_proj.shape[1], latent_proj.shape[1]
    n_e = expand_proj.shape[1] // groups
    experts_count = 16
    capacity = 3 * toks * TOPK // (2 * experts_count)

    chosen = routes[0]
    levels = gate_levels[0]
    by_expert = jnp.sum(
        jnp.where(
            chosen.T[:, None, :] == jnp.arange(experts_count, dtype=jnp.int32)[None, :, None],
            levels.T[:, None, :],
            0,
        ),
        axis=0,
    )
    line = lambda v: jnp.pad(v, (0, toks - v.shape[0]))[None]
    info = jnp.concatenate(
        [
            by_expert.astype(bf),
            jnp.sum(levels, axis=1).astype(bf)[None],
            line(norm_gain),
            line(mixer_gain),
            line(latent_gain),
            jnp.zeros((rows - experts_count - 4, toks), bf),
        ],
        axis=0,
    )
    folded = jnp.concatenate(jnp.split(expand_proj, groups, axis=1), axis=0)
    aside = n_q + n_e + n_o + 5 * toks
    wide = 6 * toks
    packed = jnp.concatenate(
        [
            query_proj,
            folded,
            output_proj,
            jnp.pad(latent_proj, ((0, 0), (0, 5 * toks - n_l))),
            info,
        ],
        axis=1,
    )
    grouped = gather_all(packed, 1)
    grouped, held_cotangent = lax.optimization_barrier((grouped, cotangent[0]))
    all_info = grouped[:, :, :, aside : aside + toks].astype(f32).reshape(n_dev, rows, toks)
    gain_one = all_info[:, experts_count + 1, :rows].reshape(-1)
    gain_two = all_info[:, experts_count + 2, :rows].reshape(-1)
    gain_latent = all_info[:, experts_count + 3, :latent_rows].reshape(-1)
    blocks = grouped.reshape(n_dev, rows, -1)
    weights = blocks.reshape(width, -1)

    n_s = shared_down.shape[0]
    lanes = 128
    fill = lambda v: jnp.pad(v.reshape(rows, n_dev, n_s), ((0, 0), (0, 0), (0, lanes - n_s)))
    gate_up = jnp.concatenate([fill(shared_gate), fill(shared_up)], axis=2)
    w_shared = lax.all_to_all(
        jnp.swapaxes(gate_up, 0, 1), both, split_axis=0, concat_axis=0, tiled=True
    ).reshape(width, 2 * lanes)

    cot_all = lax.all_gather(held_cotangent, both, axis=0, tiled=True)

    normed = norm_apply(inputs, gain_one).astype(bf)
    query_raw = times_columns(normed, weights, 0, n_q // 512, 512).reshape(toks, H, DN + DR)
    latent_raw = times_columns(normed, weights, (n_q + n_e + n_o) // wide, 1, wide)[:, :n_l]
    latent = latent_raw[:, :KVL]
    latent_normed = norm_apply(latent, gain_latent).astype(bf)
    positions = seq * toks + jnp.arange(toks, dtype=jnp.int32)
    cosine, sine = rotary_tables(positions, DR)
    query = jnp.concatenate(
        [query_raw[:, :, :DN], rotate(query_raw[:, :, DN:], cosine[:, None, :], sine[:, None, :])],
        axis=2,
    ).astype(bf)
    key_rotary = rotate(latent_raw[:, KVL:], cosine, sine).astype(bf)
    own = jnp.concatenate([latent_normed, key_rotary, jnp.zeros((toks, 64), bf)], axis=1)
    pair = seq_swap(jnp.stack([own, own]), 4)
    pair = jnp.where(seq == 0, pair, pair[::-1]).reshape(2 * toks, -1)
    latent_full = pair[:, :KVL]
    rotary_full = pair[:, KVL : KVL + DR]
    expanded = times_folded(latent_full, blocks, latent_rows, n_q // n_e, n_e)
    expanded = expanded.reshape(2 * toks, H, DN + DV)
    keys, values = expanded[:, :, :DN], expanded[:, :, DN:]
    keys = jnp.concatenate(
        [keys, jnp.broadcast_to(rotary_full[:, None, :], (2 * toks, H, DR))], axis=2
    )
    documents = jnp.cumsum(doc_starts[0])
    key_spots = jnp.arange(2 * toks)
    own_documents = lax.dynamic_slice(documents, (seq * toks,), (toks,))
    allowed = (key_spots[None, :] <= positions[:, None]) & (
        documents[None, :] == own_documents[:, None]
    )
    score_scale = (DN + DR) ** (-0.5)
    scores = jnp.einsum("qhd,khd->hqk", query, keys, preferred_element_type=f32) * score_scale
    scores = jnp.where(allowed[None], scores, -1e30)
    raised = jnp.exp(scores - jnp.max(scores, axis=-1, keepdims=True))
    soft = raised / jnp.sum(raised, axis=-1, keepdims=True)
    soft_low = soft.astype(bf)
    mixed = jnp.einsum("hqk,khd->qhd", soft_low, values, preferred_element_type=f32).astype(bf)
    attended = mixed.reshape(toks, H * DV)
    middle = inputs + times_columns(attended, weights, (n_q + n_e) // 512, n_o // 512, 512)
    normed_two = norm_apply(middle, gain_two).astype(bf)

    gathered = gather_all(normed_two, 5)
    x_all = gathered.reshape(-1, width)
    level = lax.dynamic_index_in_dim(all_info, fsdp, axis=1, keepdims=False)
    mask = level > 0
    share = level / all_info[:, experts_count]
    slot = jnp.cumsum(mask.astype(jnp.int32), axis=1) - 1
    pair = lambda v: v.reshape(n_dev // 2, 2 * toks)
    slot = pair(slot + capacity * (jnp.arange(n_dev, dtype=jnp.int32)[:, None] % 2))
    pick = pair(mask)[:, None, :] & (
        slot[:, None, :] == jnp.arange(2 * capacity, dtype=jnp.int32)[None, :, None]
    )
    pick = pick.astype(bf)
    pair_share = pair(share)[:, None, :]
    weights_here = (
        expert_gate[0].T,
        expert_up[0].T,
        expert_down[0],
        w_shared,
        jnp.pad(shared_down, ((0, lanes - n_s), (0, 0))),
    )
    n_rows, n_h, steps = n_dev * capacity, expert_gate.shape[2], n_dev // 4
    out_parts, e_rows, e_pre, e_lift, e_hidden, s_both, s_hidden = by_tiles(
        forward_kernel,
        "experts_forward",
        40,
        (x_all, pick, pair_share),
        weights_here,
        (
            ((n_dev * toks, width), bf),
            ((n_rows, width), bf),
            ((n_rows, n_h), f32),
            ((n_rows, n_h), f32),
            ((n_rows, n_h), bf),
            ((n_dev * toks, 2 * lanes), f32),
            ((n_dev * toks, lanes), bf),
        ),
        steps,
    )
    layer_out = middle + lax.psum_scatter(
        out_parts, both, scatter_dimension=0, tiled=True
    ).astype(f32)
    grad_out = cotangent[0].astype(f32)
    d_parts, d_rows, d_pre, d_lift, d_shared = by_tiles(
        backward_kernel,
        "experts_backward",
        50,
        (cot_all, pick, pair_share, e_pre, e_lift, s_both),
        weights_here,
        (
            ((n_dev * toks, width), bf),
            ((n_rows, width), bf),
            ((n_rows, n_h), bf),
            ((n_rows, n_h), bf),
            ((n_dev * toks, 2 * lanes), bf),
        ),
        steps,
    )
    expert_down_grad = contract(e_hidden, d_rows, 0, 0)
    expert_gate_grad = contract(e_rows, d_pre, 0, 0)
    expert_up_grad = contract(e_rows, d_lift, 0, 0)
    shared_down_grad = contract(s_hidden, cot_all, 0, 0)[:n_s]
    shared_both_grad = contract(x_all, d_shared, 0, 0).astype(bf)
    expert_down_grad, expert_gate_grad, expert_up_grad, shared_down_grad, shared_both_grad, d_parts = (
        lax.optimization_barrier(
            (
                expert_down_grad,
                expert_gate_grad,
                expert_up_grad,
                shared_down_grad,
                shared_both_grad,
                d_parts,
            )
        )
    )
    d_normed_two = scatter_sum(d_parts.reshape(n_dev, toks, width), 7)
    shared_back = lax.all_to_all(
        shared_both_grad.reshape(n_dev, rows, 256), both, split_axis=0, concat_axis=0, tiled=True
    )
    shared_back = jnp.swapaxes(shared_back, 0, 1).astype(f32)
    shared_gate_grad = shared_back[:, :, :n_s].reshape(rows, n_dev * n_s)
    shared_up_grad = shared_back[:, :, lanes : lanes + n_s].reshape(rows, n_dev * n_s)

    d_middle_norm, mixer_gain_grad = norm_back(middle, gain_two, d_normed_two)
    d_middle = grad_out + d_middle_norm
    d_attn = d_middle.astype(bf)
    d_mixed = times_rows(d_attn, weights, (n_q + n_e) // n_o, n_o, 512).astype(bf).reshape(toks, H, DV)
    d_soft = jnp.einsum("qhd,khd->hqk", d_mixed, values, preferred_element_type=f32)
    delta = jnp.sum(soft * d_soft, axis=-1, keepdims=True)
    d_scores = (soft * (d_soft - delta)).astype(bf)
    d_values = jnp.einsum("hqk,qhd->khd", soft_low, d_mixed, preferred_element_type=f32).astype(bf)
    d_query = (
        jnp.einsum("hqk,khd->qhd", d_scores, keys, preferred_element_type=f32) * score_scale
    )
    d_keys = (
        jnp.einsum("hqk,qhd->khd", d_scores, query, preferred_element_type=f32) * score_scale
    )
    d_query_raw = (
        jnp.concatenate(
            [
                d_query[:, :, :DN],
                rotate(d_query[:, :, DN:], cosine[:, None, :], -sine[:, None, :]),
            ],
            axis=2,
        )
        .astype(bf)
        .reshape(toks, -1)
    )
    d_expanded = jnp.concatenate([d_keys[:, :, :DN].astype(bf), d_values], axis=2)
    d_expanded = d_expanded.reshape(2 * toks, -1)
    d_latent_pair = times_folded_back(d_expanded, blocks, latent_rows, n_q // n_e, n_e)
    d_rotary_pair = jnp.sum(d_keys[:, :, DN:], axis=1)
    d_pair = jnp.concatenate(
        [d_latent_pair, d_rotary_pair, jnp.zeros((2 * toks, 64), f32)], axis=1
    ).reshape(2, toks, -1)
    d_pair = jnp.sum(seq_swap(d_pair.astype(bf), 8).astype(f32), axis=0)
    d_latent_normed = d_pair[:, :KVL]
    d_key_rotary = rotate(d_pair[:, KVL : KVL + DR], cosine, -sine)
    d_latent, latent_gain_grad = norm_back(latent, gain_latent, d_latent_normed)
    d_latent_raw = jnp.concatenate([d_latent, d_key_rotary], axis=1).astype(bf)
    d_latent_wide = jnp.pad(d_latent_raw, ((0, 0), (0, wide - n_l)))
    d_normed = times_rows(d_query_raw, weights, 0, n_q, 512) + times_rows(
        d_latent_wide, weights, (n_q + n_e + n_o) // wide, wide, 512
    )
    d_inputs, norm_gain_grad = norm_back(inputs, gain_one, d_normed)
    input_grad = d_middle + d_inputs

    latent_gain_part = jnp.pad(
        latent_gain_grad.reshape(n_dev, latent_rows), ((0, 0), (0, rows - latent_rows))
    )
    gain_parts = jnp.stack(
        [
            norm_gain_grad.reshape(n_dev, rows),
            mixer_gain_grad.reshape(n_dev, rows),
            latent_gain_part,
        ],
        axis=2,
    )
    gain_parts = jnp.pad(gain_parts, ((0, 0), (0, 0), (n_l, wide - n_l - 3))).astype(bf)
    grad_parts = packed_grads(
        n_dev,
        rows,
        latent_rows,
        normed.T,
        d_query_raw,
        latent_full.T,
        d_expanded,
        attended.T,
        d_attn,
        d_latent_wide,
        gain_parts,
    )
    grads = scatter_sum(grad_parts, 9)
    at_output = n_q + n_e
    at_latent = at_output + n_o
    at_gain = at_latent + n_l
    expand_out = jnp.concatenate(
        jnp.split(grads[:, n_q:at_output], groups, axis=0), axis=1
    )
    return (
        layer_out[None],
        input_grad[None],
        grads[:, at_gain],
        grads[:, :n_q],
        grads[:, at_latent:at_gain],
        grads[:latent_rows, at_gain + 2],
        expand_out,
        grads[:, at_output:at_latent],
        grads[:, at_gain + 1],
        shared_gate_grad,
        shared_up_grad,
        shared_down_grad,
        expert_gate_grad[None],
        expert_up_grad[None],
        expert_down_grad[None],
    )


def plain_body(
    tokens,
    norm_gain,
    query_proj,
    latent_proj,
    latent_gain,
    expand_proj,
    output_proj,
    mixer_gain,
    shared_gate,
    shared_up,
    shared_down,
    expert_gate,
    expert_up,
    expert_down,
    doc_starts,
    routes,
    gate_levels,
    cotangent,
):
    params = (
        norm_gain,
        query_proj,
        latent_proj,
        latent_gain,
        expand_proj,
        output_proj,
        mixer_gain,
        shared_gate,
        shared_up,
        shared_down,
        expert_gate,
        expert_up,
        expert_down,
    )
    saved = forward(params, tokens, doc_starts, routes, gate_levels)
    layer_out = saved["output"]
    input_grad, reduced, expert_gate_grad, expert_up_grad, expert_down_grad = backward(
        saved, cotangent
    )
    return (
        layer_out[None],
        input_grad[None],
        reduced[0],
        reduced[1],
        reduced[2],
        reduced[3],
        reduced[4],
        reduced[5],
        reduced[6],
        reduced[7],
        reduced[8],
        reduced[9],
        expert_gate_grad[None],
        expert_up_grad[None],
        expert_down_grad[None],
    )


def solution(mesh):
    in_specs = (
        P("fsdp", "seq", None),
        P(("seq", "fsdp")),
        P(("seq", "fsdp"), None),
        P(("seq", "fsdp"), None),
        P(("seq", "fsdp")),
        P(("seq", "fsdp"), None),
        P(("seq", "fsdp"), None),
        P(("seq", "fsdp")),
        P(("seq", "fsdp"), None),
        P(("seq", "fsdp"), None),
        P(("seq", "fsdp"), None),
        P("fsdp", None, "seq"),
        P("fsdp", None, "seq"),
        P("fsdp", "seq", None),
        P("fsdp", None),
        P("fsdp", "seq", None),
        P("fsdp", "seq", None),
        P("fsdp", "seq", None),
    )
    out_specs = (
        P("fsdp", "seq", None),
        P("fsdp", "seq", None),
        P(("seq", "fsdp")),
        P(("seq", "fsdp"), None),
        P(("seq", "fsdp"), None),
        P(("seq", "fsdp")),
        P(("seq", "fsdp"), None),
        P(("seq", "fsdp"), None),
        P(("seq", "fsdp")),
        P(("seq", "fsdp"), None),
        P(("seq", "fsdp"), None),
        P(("seq", "fsdp"), None),
        P("fsdp", None, "seq"),
        P("fsdp", None, "seq"),
        P("fsdp", "seq", None),
    )
    chosen = block_body if dict(mesh.shape) == {"seq": 2, "fsdp": 16} else plain_body
    return jax.shard_map(chosen, mesh=mesh, in_specs=in_specs, out_specs=out_specs, check_vma=False)
```
